128 devices in a mesh: dp: 2 (over z_hi), ctx: 64 (over y, z_lo, x, core).
Axes of the slice: x: 4, y: 4, z: 4 (z_hi: 2, z_lo: 2; z = z_hi * 2 + z_lo), core: 2. Of those that a mesh axis runs over, the one named last changes fastest.
Arguments:
- query: bfloat16 [8192, 16384], P(None, ('dp', 'ctx')), may hold values from -6 to 6
- key_in: bfloat16 [8192, 16384], P(None, ('dp', 'ctx')), may hold values from -6 to 6
- value_in: bfloat16 [8192, 16384], P(None, ('dp', 'ctx')), may hold values from -6 to 6
- cotangent: bfloat16 [8192, 16384], P(None, ('dp', 'ctx')), may hold values from -6 to 6
- residue: float32 [8192, 16], P('ctx'), may hold values from -4 to 4
- log_rate: float32 [8192, 16], P('ctx'), as said below
- bias: float32 [8192], P('ctx'), may hold values from 0.25 to 1.5
Outputs:
- gated: bfloat16 [8192, 16384], P(None, ('dp', 'ctx'))
- grad_query: bfloat16 [8192, 16384], P(None, ('dp', 'ctx'))
- grad_key: bfloat16 [8192, 16384], P(None, ('dp', 'ctx'))
- grad_value: bfloat16 [8192, 16384], P(None, ('dp', 'ctx'))
- grad_residue: float32 [8192, 16], P('ctx')
- grad_log_rate: float32 [8192, 16], P('ctx')
- grad_bias: float32 [8192], P('ctx')
The draws below stay inside these ranges and needn't reach their ends.
Inputs may be any that keep to these rules, and one draw needn't show every extreme that they name: exp(log_rate) lies between 0.1 / 8192 and 1 / 30.
All inputs are finite; a program needn't handle non-finite values.
Results may differ from the reference program's by a relative error of at most 0.0065.
Values may be sent and summed in bfloat16 or wider, within the bound.
A program may use at most 128 MiB of HBM per device.

```python
import math
import jax
import jax.numpy as jnp
from jax import lax

C = 8192
RANK = 16
SEQ = 8192
TOKENS = 16384


def spread_log(key, lower, upper):
    low_log = math.log(lower)
    high_log = math.log(upper)
    return low_log + jax.random.uniform(key, (C, RANK), jnp.float32) * (high_log - low_log)


def draw_log_rate(key, part):
    key = jax.random.fold_in(key, 7)
    pick_key, slow_key, middle_key, fast_key = jax.random.split(key, 4)
    slow_share = 0.2
    fast_share = 0.1
    slow_lower = 0.3
    slow_part = spread_log(slow_key, slow_lower / SEQ, 2.0 / SEQ)
    middle_part = spread_log(middle_key, max(1.0 / 1500.0, 0.2 / SEQ), 1.0 / 120.0)
    fast_part = spread_log(fast_key, 1.0 / 50.0, 1.0 / 30.0)
    picked = jax.random.uniform(pick_key, (C, RANK), jnp.float32)
    chosen = jnp.where(picked < slow_share, slow_part, jnp.where(picked > 1.0 - fast_share, fast_part, middle_part))
    return chosen.astype(jnp.float32)


def level_of(key, shape, cuts, least, high):
    loudness, own = 1.0, jax.random.fold_in(key, 6)
    for dim, parts in cuts:
        draws = jnp.exp(jax.random.uniform(jax.random.fold_in(own, dim), (parts,), jnp.float32, least / len(cuts), high / len(cuts)))
        loudness = loudness * jnp.repeat(draws, shape[dim] // parts).reshape([-1 if axis == dim else 1 for axis in range(len(shape))])
    return loudness


def normal_values(key, shape, deviation, most, pieces=(), held_as=jnp.bfloat16):
    drawn = deviation * jax.random.normal(key, shape, jnp.float32)
    if pieces:
        drawn = drawn * level_of(key, shape, pieces, -0.22, 0.18)
    return jnp.clip(drawn, -most, most).astype(held_as)


def setup_inputs(seed: int = 0) -> dict:
    seeds = jax.random.split(jax.random.key(seed), 8)
    query = normal_values(seeds[0], (C, TOKENS), 1.0, 6.0, ((1, 128),))
    key_in = normal_values(seeds[1], (C, TOKENS), 1.0, 6.0, ((1, 128),))
    value_in = normal_values(seeds[2], (C, TOKENS), 1.0, 6.0, ((1, 128),))
    cotangent = normal_values(seeds[3], (C, TOKENS), 1.0, 6.0, ((1, 128),))
    residue = normal_values(seeds[4], (C, RANK), 0.25, 4.0, ((0, 64),), jnp.float32)
    log_rate = draw_log_rate(jax.random.fold_in(seeds[7], 71), 0)
    bias = jnp.clip(0.25 + 1.25 * jax.random.uniform(seeds[6], (C,), jnp.float32) ** level_of(seeds[6], (C,), ((0, 64),), -0.2, 0.2), 0.25, 1.5)
    return dict(query=query, key_in=key_in, value_in=value_in, cotangent=cotangent, residue=residue, log_rate=log_rate, bias=bias)


def reference(query, key_in, value_in, cotangent, residue, log_rate, bias):
    channels, tokens = query.shape
    groups = tokens // SEQ
    product = (key_in.astype(jnp.float32) * value_in.astype(jnp.float32)).astype(jnp.bfloat16)
    mixed_grad = (cotangent.astype(jnp.float32) * query.astype(jnp.float32)).astype(jnp.bfloat16)
    block_size = min(256, channels)
    block_count = channels // block_size
    positions = jnp.arange(SEQ, dtype=jnp.float32)

    def filter_taps(residues, rates_log):
        decay_rate = jnp.exp(rates_log)
        gain_scale = residues * jnp.sqrt(-jnp.expm1(-2.0 * decay_rate))
        modes = jnp.exp(-decay_rate[:, :, None] * positions)
        return jnp.einsum('cr,crt->ct', gain_scale, modes, precision=lax.Precision.HIGHEST)

    def convolve(signal, residues, rates_log):
        spectrum = jnp.fft.rfft(signal, n=2 * SEQ, axis=-1)
        filter_spec = jnp.fft.rfft(filter_taps(residues, rates_log), n=2 * SEQ, axis=-1)
        return jnp.fft.irfft(spectrum * filter_spec[:, None, :], n=2 * SEQ, axis=-1)[..., :SEQ]

    def one_block(packed):
        signal, grad_in, residues, rates_log, skip_gain = packed
        output, pullback = jax.vjp(convolve, signal, residues, rates_log)
        d_signal, d_residue, d_rate = pullback(grad_in)
        mixed = (output + skip_gain[:, None, None] * signal).astype(jnp.bfloat16)
        back_grad = (d_signal + skip_gain[:, None, None] * grad_in).astype(jnp.bfloat16)
        return (mixed, back_grad, d_residue, d_rate, lax.optimization_barrier(jnp.sum(grad_in * signal, axis=(1, 2))))
    signal_blocks = product.astype(jnp.float32).reshape(block_count, block_size, groups, SEQ)
    grad_blocks = mixed_grad.astype(jnp.float32).reshape(block_count, block_size, groups, SEQ)
    packed = (signal_blocks, grad_blocks, residue.reshape(block_count, block_size, -1), log_rate.reshape(block_count, block_size, -1), bias.reshape(block_count, block_size))
    mixed, back_grad, d_residue, d_rate, d_bias = lax.map(one_block, packed)
    mixed = mixed.reshape(channels, tokens)
    back_grad = back_grad.reshape(channels, tokens)
    norm_scale = 1.0 / jnp.sqrt(jnp.float32(tokens))
    gated = (query.astype(jnp.float32) * mixed.astype(jnp.float32)).astype(jnp.bfloat16)
    grad_query = (cotangent.astype(jnp.float32) * mixed.astype(jnp.float32)).astype(jnp.bfloat16)
    grad_key = (back_grad.astype(jnp.float32) * value_in.astype(jnp.float32)).astype(jnp.bfloat16)
    grad_value = (back_grad.astype(jnp.float32) * key_in.astype(jnp.float32)).astype(jnp.bfloat16)
    grad_residue = d_residue.reshape(channels, -1) * norm_scale
    grad_log_rate = d_rate.reshape(channels, -1) * norm_scale
    grad_bias = d_bias.reshape(channels) * norm_scale
    return (gated, grad_query, grad_key, grad_value, grad_residue, grad_log_rate, grad_bias)
```

```python
import functools
import math

import jax
import jax.numpy as jnp
import numpy as np
from jax import lax
from jax.experimental import pallas as pl
from jax.experimental.pallas import tpu as pltpu
from jax.sharding import PartitionSpec as P

bf16 = jnp.bfloat16
f32 = jnp.float32
W = 128
HALF = 8
LANES = 256


def tables():
    n = np.arange(W)[:, None]
    f = np.arange(W)[None, :]
    angle = ((2 * f + 1) * n % (4 * W)) * (2.0 * math.pi / (4 * W))
    fwd = np.concatenate([np.cos(angle), -np.sin(angle)], axis=1)
    inv = fwd.T / W
    flip = np.eye(W)[::-1]
    cast = lambda z: jnp.asarray(np.ascontiguousarray(z), f32).astype(bf16)
    return cast(fwd), cast(fwd[::-1]), cast(inv), cast(inv[:, ::-1]), cast(flip)


def dot(a, b):
    return jnp.dot(a, b, preferred_element_type=f32)


def dot_nt(a, b):
    return lax.dot_general(a, b, (((1,), (1,)), ((), ())), preferred_element_type=f32)


def powers(rate_row):
    rate8 = jnp.broadcast_to(rate_row, (8, LANES))
    row = lax.broadcasted_iota(jnp.int32, (8, LANES), 0).astype(f32)
    out = jnp.exp(-rate8 * row)
    for step in (8, 16, 32, 64):
        mult = jnp.exp(-rate8 * float(step))
        parts = [out[i : i + 8] * mult for i in range(0, step, 8)]
        out = jnp.concatenate([out] + parts, axis=0)
    return out.astype(bf16)


def diag_mask():
    row = lax.broadcasted_iota(jnp.int32, (16, LANES), 0)
    lane = lax.broadcasted_iota(jnp.int32, (16, LANES), 1)
    return row == lane // 16


def diag_row(mask, rows):
    return jnp.sum(jnp.where(mask, rows, 0.0), axis=0, keepdims=True)


def mul16(a, b):
    return (a.astype(f32) * b.astype(f32)).astype(bf16)


def states_kernel(q_ref, k_ref, v_ref, c_ref, par_ref, flip_ref, out_ref):
    mask = diag_mask()

    def step(i, carry):
        sl = pl.ds(pl.multiple_of(i * 128, 128), 128)
        x = mul16(k_ref[sl, :], v_ref[sl, :])
        m = mul16(c_ref[sl, :], q_ref[sl, :])
        xr = dot(x, flip_ref[...]).astype(bf16)
        ahead, back = [], []
        for g in range(HALF):
            e = powers(par_ref[i, g : g + 1, :])
            rows = slice(16 * g, 16 * g + 16)
            res = dot(jnp.concatenate([xr[rows], m[rows]], axis=0), e)
            ahead.append(diag_row(mask, res[:16]))
            back.append(diag_row(mask, res[16:]))
        out_ref[i] = jnp.concatenate(ahead + back, axis=0).astype(bf16)
        return carry

    lax.fori_loop(0, out_ref.shape[0], step, 0)


def scan_kernel(st_ref, rate_ref, out_ref, hold):
    parts = st_ref.shape[0]
    decay = jnp.exp(-float(W) * rate_ref[...])

    def ahead(p, s):
        hold[p] = s
        return s * decay + st_ref[p].astype(f32)[:HALF]

    lax.fori_loop(0, parts, ahead, jnp.zeros((HALF, LANES), f32))

    def back(i, s):
        p = parts - 1 - i
        out_ref[p] = jnp.concatenate([hold[p], s], axis=0).astype(bf16)
        return s * decay + st_ref[p].astype(f32)[HALF:]

    lax.fori_loop(0, parts, back, jnp.zeros((HALF, LANES), f32))


def cmul(a, b):
    ar, ai, br, bi = a[:, :W], a[:, W:], b[:, :W], b[:, W:]
    return jnp.concatenate([ar * br - ai * bi, ar * bi + ai * br], axis=1).astype(bf16)


def mix_kernel(
    q_ref, k_ref, v_ref, c_ref, par_ref, own_ref, st_ref, fwd_ref, fwdr_ref, inv_ref, invr_ref,
    flip_ref, gated_ref, gq_ref, gk_ref, gv_ref, grad_ref, taps_s, yc_s, pc_s,
):
    mask = diag_mask()
    eye = lax.broadcasted_iota(jnp.int32, (W, W), 0) == lax.broadcasted_iota(jnp.int32, (W, W), 1)
    lag_no = lax.broadcasted_iota(jnp.int32, (W, W), 1).astype(f32)

    def step(i, carry):
        sl = pl.ds(pl.multiple_of(i * 128, 128), 128)
        q, k, v, c = q_ref[sl, :], k_ref[sl, :], v_ref[sl, :], c_ref[sl, :]
        x, m = mul16(k, v), mul16(c, q)
        xf, mf = x.astype(f32), m.astype(f32)
        xr = dot(x, flip_ref[...])
        spec_x = dot(x, fwd_ref[...])
        spec_m = dot(m, fwdr_ref[...])
        lag = dot(cmul(spec_x, spec_m), invr_ref[...])
        lag0 = lag.astype(bf16)
        lag1 = (lag * lag_no).astype(bf16)
        m1 = (mf * (lag_no + 1.0)).astype(bf16)
        x1 = (xr * lag_no).astype(bf16)
        rate = par_ref[i, 0:8, :]
        weight = par_ref[i, 8:16, :]
        state = st_ref[i].astype(f32)
        ahead, back = state[:HALF], state[HALF:]
        local_b = own_ref[i].astype(f32)[HALF:]
        decay = jnp.exp(-rate)
        wa = weight * decay * ahead
        wb = weight * decay * back
        a_rows, d_rows, m_rows, x_rows = [], [], [], []
        for g in range(HALF):
            e = powers(rate[g : g + 1])
            rows = slice(16 * g, 16 * g + 16)
            lhs = jnp.concatenate(
                [
                    jnp.where(mask, weight[g : g + 1], 0.0),
                    jnp.where(mask, wa[g : g + 1], 0.0),
                    jnp.where(mask, wb[g : g + 1], 0.0),
                ],
                axis=0,
            ).astype(bf16)
            z = dot_nt(lhs, e)
            taps_s[rows, :] = z[:16]
            yc_s[rows, :] = z[16:32]
            pc_s[rows, :] = z[32:]
            res = dot(jnp.concatenate([lag0[rows], lag1[rows], m1[rows], x1[rows]], axis=0), e)
            a_rows.append(diag_row(mask, res[:16]))
            d_rows.append(diag_row(mask, res[16:32]))
            m_rows.append(diag_row(mask, res[32:48]))
            x_rows.append(diag_row(mask, res[48:]))
        grad_a = jnp.concatenate(a_rows, axis=0) + decay * local_b * ahead
        grad_d = (
            jnp.concatenate(d_rows, axis=0)
            + float(W) * jnp.exp(-float(W + 1) * rate) * ahead * back
            + decay * ahead * jnp.concatenate(m_rows, axis=0)
            + decay * back * jnp.concatenate(x_rows, axis=0)
        )
        skip_sum = jnp.sum(xf * mf, axis=1, keepdims=True)
        skip_row = jnp.sum(jnp.where(eye, skip_sum, 0.0), axis=0, keepdims=True)
        skip_part = jnp.concatenate(
            [jnp.broadcast_to(skip_row, (16, W)), jnp.zeros((16, W), f32)], axis=1
        )
        grad_ref[i] = jnp.concatenate([grad_a, grad_d, skip_part], axis=0).astype(bf16)
        skip_gain = jnp.sum(
            jnp.where(eye, par_ref[i, 16:17, :W], 0.0), axis=1, keepdims=True
        )
        spec_h = dot(taps_s[...].astype(bf16), fwd_ref[...])
        y = dot(cmul(spec_x, spec_h), inv_ref[...]) + yc_s[...] + skip_gain * xf
        p = (
            dot(cmul(spec_m, spec_h), invr_ref[...])
            + dot(pc_s[...].astype(bf16), flip_ref[...])
            + skip_gain * mf
        )
        mixed = y.astype(bf16)
        pgrad = p.astype(bf16)
        gated_ref[sl, :] = mul16(q, mixed)
        gq_ref[sl, :] = mul16(c, mixed)
        gk_ref[sl, :] = mul16(pgrad, v)
        gv_ref[sl, :] = mul16(pgrad, k)
        return carry

    lax.fori_loop(0, grad_ref.shape[0], step, 0)


def body(query, key_in, value_in, cotangent, residue, log_rate, bias):
    shards = lax.axis_size("ctx")
    channels, width = query.shape
    fwd, fwdr, inv, invr, flip = tables()
    rate = jnp.exp(log_rate)
    root = jnp.sqrt(-jnp.expm1(-2.0 * rate))
    rate_rows = rate.reshape(HALF, LANES)
    weight_rows = (residue * root).reshape(HALF, LANES)
    bias_rows = jnp.pad(bias.reshape(1, W), ((0, 7), (0, LANES - W)))
    own_par = jnp.concatenate([rate_rows, weight_rows, bias_rows], axis=0)
    par = lax.all_gather(own_par, "ctx")

    sub = 4
    block = sub * 128
    grid = (channels // block,)
    data = pl.BlockSpec((block, width), lambda i: (i, 0))
    rows24 = pl.BlockSpec((sub, 24, LANES), lambda i: (i, 0, 0))
    rows16 = pl.BlockSpec((sub, 16, LANES), lambda i: (i, 0, 0))
    rows32 = pl.BlockSpec((sub, 32, LANES), lambda i: (i, 0, 0))
    whole = lambda r, c: pl.BlockSpec((r, c), lambda i: (0, 0))
    params = pltpu.CompilerParams(vmem_limit_bytes=48 * 1024 * 1024)

    own_states = pl.pallas_call(
        states_kernel,
        grid=grid,
        in_specs=[data] * 4 + [rows24, whole(W, W)],
        out_specs=rows16,
        out_shape=jax.ShapeDtypeStruct((shards, 16, LANES), bf16),
        compiler_params=params,
        name="states",
    )(query, key_in, value_in, cotangent, par, flip)

    gathered = lax.all_to_all(own_states, "ctx", split_axis=0, concat_axis=0, tiled=True)
    scanned = pl.pallas_call(
        scan_kernel,
        out_shape=jax.ShapeDtypeStruct((shards, 16, LANES), bf16),
        scratch_shapes=[pltpu.VMEM((shards, HALF, LANES), f32)],
        compiler_params=params,
        name="scan",
    )(gathered, rate_rows)
    states = lax.all_to_all(scanned, "ctx", split_axis=0, concat_axis=0, tiled=True)

    out = jax.ShapeDtypeStruct((channels, width), bf16)
    gated, gq, gk, gv, grads = pl.pallas_call(
        mix_kernel,
        grid=grid,
        in_specs=[data] * 4
        + [rows24, rows16, rows16, whole(W, 2 * W), whole(W, 2 * W), whole(2 * W, W),
           whole(2 * W, W), whole(W, W)],
        out_specs=[data] * 4 + [rows32],
        out_shape=[out] * 4 + [jax.ShapeDtypeStruct((shards, 32, LANES), bf16)],
        scratch_shapes=[pltpu.VMEM((W, W), f32)] * 3,
        compiler_params=params,
        name="mix",
    )(query, key_in, value_in, cotangent, par, own_states, states, fwd, fwdr, inv, invr, flip)

    parts = lax.all_to_all(grads, "ctx", split_axis=0, concat_axis=0, tiled=True)
    total = lax.psum(jnp.sum(parts.astype(f32), axis=0)[:24], "dp")
    modes = residue.shape[1]
    grad_a = total[:HALF].reshape(-1, modes)
    grad_d = total[HALF:16].reshape(-1, modes)
    scale = 1.0 / math.sqrt(float(shards * width * lax.axis_size("dp")))
    grad_residue = root * grad_a * scale
    grad_rate = rate * residue * (jnp.exp(-2.0 * rate) / root * grad_a - root * grad_d) * scale
    grad_bias = total[16, :W] * scale
    return gated, gq, gk, gv, grad_residue, grad_rate, grad_bias


def solution(mesh):
    tok = P(None, ("dp", "ctx"))
    chan = P("ctx", None)
    return jax.shard_map(
        body,
        mesh=mesh,
        in_specs=(tok, tok, tok, tok, chan, chan, P("ctx")),
        out_specs=(tok, tok, tok, tok, chan, chan, P("ctx")),
        check_vma=False,
    )
```

```python
import functools
import math

import jax
import jax.numpy as jnp
import numpy as np
from jax import lax
from jax.experimental import pallas as pl
from jax.experimental.pallas import tpu as pltpu
from jax.sharding import PartitionSpec as P

bf16 = jnp.bfloat16
f32 = jnp.float32
W = 128
HALF = 8
LANES = 256


def tables():
    n = np.arange(W)[:, None]
    f = np.arange(W)[None, :]
    angle = ((2 * f + 1) * n % (4 * W)) * (2.0 * math.pi / (4 * W))
    fwd = np.concatenate([np.cos(angle), -np.sin(angle)], axis=1)
    inv = fwd.T / W
    flip = np.eye(W)[::-1]
    cast = lambda z: jnp.asarray(np.ascontiguousarray(z), f32).astype(bf16)
    return cast(fwd), cast(fwd[::-1]), cast(inv), cast(inv[:, ::-1]), cast(flip)


def dot(a, b):
    return jnp.dot(a, b, preferred_element_type=f32)


def dot_nt(a, b):
    return lax.dot_general(a, b, (((1,), (1,)), ((), ())), preferred_element_type=f32)


def powers(rate_row):
    rate8 = jnp.broadcast_to(rate_row, (8, LANES))
    row = lax.broadcasted_iota(jnp.int32, (8, LANES), 0).astype(f32)
    out = jnp.exp(-rate8 * row)
    for step in (8, 16, 32, 64):
        mult = jnp.exp(-rate8 * float(step))
        parts = [out[i : i + 8] * mult for i in range(0, step, 8)]
        out = jnp.concatenate([out] + parts, axis=0)
    return out.astype(bf16)


def diag_mask():
    row = lax.broadcasted_iota(jnp.int32, (16, LANES), 0)
    lane = lax.broadcasted_iota(jnp.int32, (16, LANES), 1)
    return row == lane // 16


def diag_row(mask, rows):
    return jnp.sum(jnp.where(mask, rows, 0.0), axis=0, keepdims=True)


def get_par(par_ref, i):
    rows = par_ref[lax.rem(i, 2), lax.div(i, 2)].astype(f32)
    return rows[:8] + rows[8:16], rows[16:24], rows[24:25, :W] + rows[25:26, :W]


def mul16(a, b):
    return (a.astype(f32) * b.astype(f32)).astype(bf16)


def states_kernel(q_ref, k_ref, v_ref, c_ref, par_ref, flip_ref, out_ref):
    mask = diag_mask()

    def step(i, carry):
        sl = pl.ds(pl.multiple_of(i * 128, 128), 128)
        x = mul16(k_ref[sl, :], v_ref[sl, :])
        m = mul16(c_ref[sl, :], q_ref[sl, :])
        xr = dot(x, flip_ref[...]).astype(bf16)
        ahead, back = [], []
        rate = get_par(par_ref, i)[0]
        for g in range(HALF):
            e = powers(rate[g : g + 1])
            rows = slice(16 * g, 16 * g + 16)
            res = dot(jnp.concatenate([xr[rows], m[rows]], axis=0), e)
            ahead.append(diag_row(mask, res[:16]))
            back.append(diag_row(mask, res[16:]))
        out_ref[i] = jnp.concatenate(ahead + back, axis=0).astype(bf16)
        return carry

    lax.fori_loop(0, out_ref.shape[0], step, 0)


def peer_of(me, d, count):
    return lax.rem(me + d, count)


def greet(offsets, me, count, extra=()):
    barrier = pltpu.get_barrier_semaphore()
    first, stop, step = offsets

    def tell(i, carry):
        pl.semaphore_signal(
            barrier, inc=1, device_id={"ctx": peer_of(me, first + i * step, count)},
            device_id_type=pl.DeviceIdType.MESH,
        )
        return carry

    number = (stop - first) // step
    lax.fori_loop(0, number, tell, 0)
    for who in extra:
        pl.semaphore_signal(barrier, inc=1, device_id=who, device_id_type=pl.DeviceIdType.MESH)
    pl.semaphore_wait(barrier, number + len(extra))


def start_all(src, dst, me, count, send_sem, recv_sem, local_sem):
    def send(d, carry):
        peer = peer_of(me, d, count)
        pltpu.make_async_remote_copy(
            src_ref=src.at[peer], dst_ref=dst.at[me], send_sem=send_sem, recv_sem=recv_sem,
            device_id={"ctx": peer}, device_id_type=pl.DeviceIdType.MESH,
        ).start()
        return carry

    lax.fori_loop(1, count, send, 0)
    return pltpu.make_async_copy(src.at[me], dst.at[me], local_sem)


def wait_bytes(ref, sem):
    pltpu.make_async_copy(ref, ref, sem).wait()


def gather_kernel(own_ref, out_ref, send_sem, recv_sem, pair_sem, local_sem):
    count = 2 * out_ref.shape[1]
    me = lax.axis_index("ctx")
    core, chip = lax.rem(me, 2), lax.div(me, 2)
    other = me + 1 - 2 * core
    greet((2, count, 2), me, count, extra=({"ctx": other},))

    def send(d, carry):
        peer = peer_of(me, 2 * d, count)
        pltpu.make_async_remote_copy(
            src_ref=own_ref, dst_ref=out_ref.at[core, chip], send_sem=send_sem, recv_sem=recv_sem,
            device_id={"ctx": peer}, device_id_type=pl.DeviceIdType.MESH,
        ).start()
        return carry

    chips = out_ref.shape[1]
    lax.fori_loop(1, chips, send, 0)
    keep = pltpu.make_async_copy(own_ref, out_ref.at[core, chip], local_sem)
    keep.start()
    keep.wait()
    some = out_ref.at[0, pl.ds(0, chips - 1)]
    wait_bytes(some, recv_sem)
    across = pltpu.make_async_remote_copy(
        src_ref=out_ref.at[core], dst_ref=out_ref.at[core], send_sem=pair_sem.at[0],
        recv_sem=pair_sem.at[1], device_id={"ctx": other}, device_id_type=pl.DeviceIdType.MESH,
    )
    across.start()
    wait_bytes(some, send_sem)
    across.wait()


def scan_kernel(
    st_ref, rate_ref, out_ref, came, ready, hold, send_sem, recv_sem, local_sem
):
    parts = st_ref.shape[0]
    me = lax.axis_index("ctx")
    greet((1, parts, 1), me, parts)
    keep = start_all(st_ref, came, me, parts, send_sem.at[0], recv_sem.at[0], local_sem.at[0])
    keep.start()
    keep.wait()
    rest = came.at[pl.ds(0, parts - 1)]
    wait_bytes(rest, recv_sem.at[0])
    decay = jnp.exp(-float(W) * rate_ref[...])

    def ahead(p, s):
        hold[p] = s
        return s * decay + came[p].astype(f32)[:HALF]

    lax.fori_loop(0, parts, ahead, jnp.zeros((HALF, LANES), f32))

    def back(i, s):
        p = parts - 1 - i
        ready[p] = jnp.concatenate([hold[p], s], axis=0).astype(bf16)
        return s * decay + came[p].astype(f32)[HALF:]

    lax.fori_loop(0, parts, back, jnp.zeros((HALF, LANES), f32))
    keep = start_all(ready, out_ref, me, parts, send_sem.at[1], recv_sem.at[1], local_sem.at[1])
    keep.start()
    wait_bytes(rest, send_sem.at[0])
    keep.wait()
    wait_bytes(out_ref.at[pl.ds(0, parts - 1)], recv_sem.at[1])
    wait_bytes(rest, send_sem.at[1])


def reduce_kernel(
    grad_ref, out_ref, came, mine, theirs, send_sem, recv_sem, local_sem, pair_sem
):
    parts = grad_ref.shape[0]
    me = lax.axis_index("ctx")
    twin = {"dp": 1 - lax.axis_index("dp")}
    greet((1, parts, 1), me, parts, extra=(twin,))
    keep = start_all(grad_ref, came, me, parts, send_sem, recv_sem, local_sem)
    keep.start()
    keep.wait()
    rest = came.at[pl.ds(0, parts - 1)]
    wait_bytes(rest, recv_sem)
    mine[...] = lax.fori_loop(
        0, parts, lambda p, s: s + came[p].astype(f32), jnp.zeros(came.shape[1:], f32)
    )
    swap = pltpu.make_async_remote_copy(
        src_ref=mine, dst_ref=theirs, send_sem=pair_sem.at[0], recv_sem=pair_sem.at[1],
        device_id=twin, device_id_type=pl.DeviceIdType.MESH,
    )
    swap.start()
    wait_bytes(rest, send_sem)
    swap.wait()
    out_ref[...] = mine[...] + theirs[...]


def cmul(a, b):
    ar, ai, br, bi = a[:, :W], a[:, W:], b[:, :W], b[:, W:]
    return jnp.concatenate([ar * br - ai * bi, ar * bi + ai * br], axis=1).astype(bf16)


def mix_kernel(
    q_ref, k_ref, v_ref, c_ref, par_ref, own_ref, st_ref, fwd_ref, fwdr_ref, inv_ref, invr_ref,
    flip_ref, gated_ref, gq_ref, gk_ref, gv_ref, grad_ref, taps_s, yc_s, pc_s,
):
    mask = diag_mask()
    eye = lax.broadcasted_iota(jnp.int32, (W, W), 0) == lax.broadcasted_iota(jnp.int32, (W, W), 1)
    lag_no = lax.broadcasted_iota(jnp.int32, (W, W), 1).astype(f32)

    def step(i, carry):
        sl = pl.ds(pl.multiple_of(i * 128, 128), 128)
        q, k, v, c = q_ref[sl, :], k_ref[sl, :], v_ref[sl, :], c_ref[sl, :]
        x, m = mul16(k, v), mul16(c, q)
        xf, mf = x.astype(f32), m.astype(f32)
        xr = dot(x, flip_ref[...])
        spec_x = dot(x, fwd_ref[...])
        spec_m = dot(m, fwdr_ref[...])
        lag = dot(cmul(spec_x, spec_m), invr_ref[...])
        lag0 = lag.astype(bf16)
        lag1 = (lag * lag_no).astype(bf16)
        m1 = (mf * (lag_no + 1.0)).astype(bf16)
        x1 = (xr * lag_no).astype(bf16)
        rate, weight, bias_row = get_par(par_ref, i)
        state = st_ref[i].astype(f32)
        ahead, back = state[:HALF], state[HALF:]
        local_b = own_ref[i].astype(f32)[HALF:]
        decay = jnp.exp(-rate)
        wa = weight * decay * ahead
        wb = weight * decay * back
        a_rows, d_rows, m_rows, x_rows = [], [], [], []
        for g in range(HALF):
            e = powers(rate[g : g + 1])
            rows = slice(16 * g, 16 * g + 16)
            lhs = jnp.concatenate(
                [
                    jnp.where(mask, weight[g : g + 1], 0.0),
                    jnp.where(mask, wa[g : g + 1], 0.0),
                    jnp.where(mask, wb[g : g + 1], 0.0),
                ],
                axis=0,
            ).astype(bf16)
            z = dot_nt(lhs, e)
            taps_s[rows, :] = z[:16]
            yc_s[rows, :] = z[16:32]
            pc_s[rows, :] = z[32:]
            res = dot(jnp.concatenate([lag0[rows], lag1[rows], m1[rows], x1[rows]], axis=0), e)
            a_rows.append(diag_row(mask, res[:16]))
            d_rows.append(diag_row(mask, res[16:32]))
            m_rows.append(diag_row(mask, res[32:48]))
            x_rows.append(diag_row(mask, res[48:]))
        grad_a = jnp.concatenate(a_rows, axis=0) + decay * local_b * ahead
        grad_d = (
            jnp.concatenate(d_rows, axis=0)
            + float(W) * jnp.exp(-float(W + 1) * rate) * ahead * back
            + decay * ahead * jnp.concatenate(m_rows, axis=0)
            + decay * back * jnp.concatenate(x_rows, axis=0)
        )
        skip_sum = jnp.sum(xf * mf, axis=1, keepdims=True)
        skip_row = jnp.sum(jnp.where(eye, skip_sum, 0.0), axis=0, keepdims=True)
        skip_part = jnp.concatenate(
            [jnp.broadcast_to(skip_row, (16, W)), jnp.zeros((16, W), f32)], axis=1
        )
        grad_ref[i] = jnp.concatenate([grad_a, grad_d, skip_part], axis=0).astype(bf16)
        skip_gain = jnp.sum(
            jnp.where(eye, bias_row, 0.0), axis=1, keepdims=True
        )
        spec_h = dot(taps_s[...].astype(bf16), fwd_ref[...])
        y = dot(cmul(spec_x, spec_h), inv_ref[...]) + yc_s[...] + skip_gain * xf
        p = (
            dot(cmul(spec_m, spec_h), invr_ref[...])
            + dot(pc_s[...].astype(bf16), flip_ref[...])
            + skip_gain * mf
        )
        mixed = y.astype(bf16)
        pgrad = p.astype(bf16)
        gated_ref[sl, :] = mul16(q, mixed)
        gq_ref[sl, :] = mul16(c, mixed)
        gk_ref[sl, :] = mul16(pgrad, v)
        gv_ref[sl, :] = mul16(pgrad, k)
        return carry

    lax.fori_loop(0, grad_ref.shape[0], step, 0)


def body(query, key_in, value_in, cotangent, residue, log_rate, bias):
    shards = lax.axis_size("ctx")
    channels, width = query.shape
    fwd, fwdr, inv, invr, flip = tables()
    rate = jnp.exp(log_rate)
    root = jnp.sqrt(-jnp.expm1(-2.0 * rate))
    rate_rows = rate.reshape(HALF, LANES)
    weight_rows = (residue * root).reshape(HALF, LANES)
    bias_row = jnp.pad(bias.reshape(1, W), ((0, 0), (0, LANES - W)))
    upper = lambda z: lax.reduce_precision(z, 8, 7)
    own_par = jnp.concatenate(
        [
            rate_rows,
            rate_rows - upper(rate_rows),
            weight_rows,
            bias_row,
            bias_row - upper(bias_row),
            jnp.zeros((6, LANES), f32),
        ],
        axis=0,
    ).astype(bf16)
    vmem = pl.BlockSpec(memory_space=pltpu.VMEM)
    dma = pltpu.SemaphoreType.DMA

    def remote(number):
        return pltpu.CompilerParams(
            collective_id=number, has_side_effects=True, vmem_limit_bytes=24 * 1024 * 1024
        )

    par = pl.pallas_call(
        gather_kernel,
        in_specs=[vmem],
        out_specs=vmem,
        out_shape=jax.ShapeDtypeStruct((2, shards // 2, 32, LANES), bf16),
        scratch_shapes=[dma, dma, dma((2,)), dma],
        compiler_params=remote(1),
        name="gather",
    )(own_par)

    sub = 4
    block = sub * 128
    grid = (channels // block,)
    data = pl.BlockSpec((block, width), lambda i: (i, 0))
    rows_par = pl.BlockSpec((2, sub // 2, 32, LANES), lambda i: (0, i, 0, 0))
    rows16 = pl.BlockSpec((sub, 16, LANES), lambda i: (i, 0, 0))
    rows32 = pl.BlockSpec((sub, 32, LANES), lambda i: (i, 0, 0))
    whole = lambda r, c: pl.BlockSpec((r, c), lambda i: (0, 0))
    params = pltpu.CompilerParams(vmem_limit_bytes=48 * 1024 * 1024)

    own_states = pl.pallas_call(
        states_kernel,
        grid=grid,
        in_specs=[data] * 4 + [rows_par, whole(W, W)],
        out_specs=rows16,
        out_shape=jax.ShapeDtypeStruct((shards, 16, LANES), bf16),
        compiler_params=params,
        name="states",
    )(query, key_in, value_in, cotangent, par, flip)

    states = pl.pallas_call(
        scan_kernel,
        in_specs=[vmem, vmem],
        out_specs=vmem,
        out_shape=jax.ShapeDtypeStruct((shards, 16, LANES), bf16),
        scratch_shapes=[
            pltpu.VMEM((shards, 16, LANES), bf16),
            pltpu.VMEM((shards, 16, LANES), bf16),
            pltpu.VMEM((shards, HALF, LANES), f32),
            dma((2,)),
            dma((2,)),
            dma((2,)),
        ],
        compiler_params=remote(2),
        name="scan",
    )(own_states, rate_rows)

    out = jax.ShapeDtypeStruct((channels, width), bf16)
    gated, gq, gk, gv, grads = pl.pallas_call(
        mix_kernel,
        grid=grid,
        in_specs=[data] * 4
        + [rows_par, rows16, rows16, whole(W, 2 * W), whole(W, 2 * W), whole(2 * W, W),
           whole(2 * W, W), whole(W, W)],
        out_specs=[data] * 4 + [rows32],
        out_shape=[out] * 4 + [jax.ShapeDtypeStruct((shards, 32, LANES), bf16)],
        scratch_shapes=[pltpu.VMEM((W, W), f32)] * 3,
        compiler_params=params,
        name="mix",
    )(query, key_in, value_in, cotangent, par, own_states, states, fwd, fwdr, inv, invr, flip)

    total = pl.pallas_call(
        reduce_kernel,
        in_specs=[vmem],
        out_specs=vmem,
        out_shape=jax.ShapeDtypeStruct((32, LANES), f32),
        scratch_shapes=[
            pltpu.VMEM((shards, 32, LANES), bf16),
            pltpu.VMEM((32, LANES), f32),
            pltpu.VMEM((32, LANES), f32),
            dma,
            dma,
            dma,
            dma((2,)),
        ],
        compiler_params=remote(3),
        name="reduce",
    )(grads)
    modes = residue.shape[1]
    grad_a = total[:HALF].reshape(-1, modes)
    grad_d = total[HALF:16].reshape(-1, modes)
    scale = 1.0 / math.sqrt(float(shards * width * lax.axis_size("dp")))
    grad_residue = root * grad_a * scale
    grad_rate = rate * residue * (jnp.exp(-2.0 * rate) / root * grad_a - root * grad_d) * scale
    grad_bias = total[16, :W] * scale
    return gated, gq, gk, gv, grad_residue, grad_rate, grad_bias


def solution(mesh):
    tok = P(None, ("dp", "ctx"))
    chan = P("ctx", None)
    return jax.shard_map(
        body,
        mesh=mesh,
        in_specs=(tok, tok, tok, tok, chan, chan, P("ctx")),
        out_specs=(tok, tok, tok, tok, chan, chan, P("ctx")),
        check_vma=False,
    )
```

```python
import functools
import math

import jax
import jax.numpy as jnp
import numpy as np
from jax import lax
from jax.experimental import pallas as pl
from jax.experimental.pallas import tpu as pltpu
from jax.sharding import PartitionSpec as P

bf16 = jnp.bfloat16
f32 = jnp.float32
W = 128
HALF = 8
MESH = pl.DeviceIdType.MESH
LANES = 256


def tables():
    n = np.arange(W)[:, None]
    f = np.arange(W)[None, :]
    angle = ((2 * f + 1) * n % (4 * W)) * (2.0 * math.pi / (4 * W))
    fwd = np.concatenate([np.cos(angle), -np.sin(angle)], axis=1)
    inv = fwd.T / W
    flip = np.eye(W)[::-1]
    cast = lambda z: jnp.asarray(np.ascontiguousarray(z), f32).astype(bf16)
    return cast(fwd), cast(fwd[::-1]), cast(inv), cast(inv[:, ::-1]), cast(flip)


def dot(a, b):
    return jnp.dot(a, b, preferred_element_type=f32)


def dot_nt(a, b):
    return lax.dot_general(a, b, (((1,), (1,)), ((), ())), preferred_element_type=f32)


def powers(rate_row):
    rate8 = jnp.broadcast_to(rate_row, (8, LANES))
    row = lax.broadcasted_iota(jnp.int32, (8, LANES), 0).astype(f32)
    out = jnp.exp(-rate8 * row)
    for step in (8, 16, 32, 64):
        mult = jnp.exp(-rate8 * float(step))
        parts = [out[i : i + 8] * mult for i in range(0, step, 8)]
        out = jnp.concatenate([out] + parts, axis=0)
    return out.astype(bf16)


def diag_mask():
    row = lax.broadcasted_iota(jnp.int32, (16, LANES), 0)
    lane = lax.broadcasted_iota(jnp.int32, (16, LANES), 1)
    return row == lane // 16


def diag_row(mask, rows):
    return jnp.sum(jnp.where(mask, rows, 0.0), axis=0, keepdims=True)


def mul16(a, b):
    return (a.astype(f32) * b.astype(f32)).astype(bf16)


def cmul(a, b):
    ar, ai, br, bi = a[:, :W], a[:, W:], b[:, :W], b[:, W:]
    return jnp.concatenate([ar * br - ai * bi, ar * bi + ai * br], axis=1).astype(bf16)


def wait_bytes(ref, sem):
    pltpu.make_async_copy(ref, ref, sem).wait()


def mixer_kernel(
    q_hbm, k_hbm, v_hbm, c_hbm, own_par, own_rate, fwd_ref, fwdr_ref, inv_ref, invr_ref, flip_ref,
    mixed_hbm, pgrad_hbm, total_ref,
    inp, away, sig, rev, lags, skip, par, keep, st_out, came, hold, ready, got, grad_out,
    grad_in, mine, theirs, expand, stage,
    load_sem, par_sem, pair_sem, st_sem, back_sem, grad_sem, out_sem, twin_sem,
):
    chips = q_hbm.shape[0]
    me = lax.axis_index("ctx")
    core, chip = lax.rem(me, 2), lax.div(me, 2)
    near = {"ctx": me + 1 - 2 * core}
    twin = {"dp": 1 - lax.axis_index("dp")}

    def peer(b):
        return {"ctx": 2 * b + core}

    def after(i):
        return lax.rem(chip + i, chips)

    def remote(src, dst, sems, who):
        return pltpu.make_async_remote_copy(
            src_ref=src, dst_ref=dst, send_sem=sems.at[0], recv_sem=sems.at[1],
            device_id=who, device_id_type=MESH,
        )

    for order in range(2):
        side = 1 - core if order == 0 else core
        for n, ref in enumerate((q_hbm, k_hbm, v_hbm, c_hbm)):
            pltpu.make_async_copy(ref.at[:, side], inp.at[order, n], load_sem.at[order]).start()

    barrier = pltpu.get_barrier_semaphore()

    def tell(i, carry):
        pl.semaphore_signal(barrier, inc=1, device_id=peer(after(i)), device_id_type=MESH)
        return carry

    lax.fori_loop(1, chips, tell, 0)
    pl.semaphore_signal(barrier, inc=1, device_id=near, device_id_type=MESH)
    pl.semaphore_signal(barrier, inc=1, device_id=twin, device_id_type=MESH)
    pl.semaphore_wait(barrier, chips + 1)

    def send_par(i, carry):
        remote(own_par, par.at[chip], par_sem, peer(after(i))).start()
        return carry

    lax.fori_loop(1, chips, send_par, 0)
    par[chip] = own_par[...]

    def products(order, dst):
        def step(b, carry):
            dst[0, b] = mul16(inp[order, 1, b], inp[order, 2, b])
            dst[1, b] = mul16(inp[order, 3, b], inp[order, 0, b])
            return carry

        lax.fori_loop(0, chips, step, 0)

    wait_bytes(inp.at[0], load_sem.at[0])
    products(0, away)
    trade = remote(away, sig.at[core], pair_sem, near)
    trade.start()
    wait_bytes(inp.at[1], load_sem.at[1])
    products(1, sig.at[core])
    trade.wait()

    eye = lax.broadcasted_iota(jnp.int32, (W, W), 0) == lax.broadcasted_iota(jnp.int32, (W, W), 1)
    lane = lax.broadcasted_iota(jnp.int32, (W, W), 1).astype(f32)
    mask = diag_mask()

    def local_lags(b, carry):
        x = jnp.concatenate([sig[0, 0, b], sig[1, 0, b]], axis=0)
        m = jnp.concatenate([sig[0, 1, b], sig[1, 1, b]], axis=0)
        xr = dot(x, flip_ref[...]).astype(bf16)
        rev[0, b] = xr[:W]
        rev[1, b] = xr[W:]
        both = dot(cmul(dot(x, fwd_ref[...]), dot(m, fwdr_ref[...])), invr_ref[...])
        lag = both[:W] + both[W:]
        lags[0, b] = lag.astype(bf16)
        lags[1, b] = (lag * lane).astype(bf16)
        xm = x.astype(f32) * m.astype(f32)
        sums = jnp.sum(xm[:W] + xm[W:], axis=1, keepdims=True)
        skip[b] = jnp.broadcast_to(
            jnp.sum(jnp.where(eye, sums, 0.0), axis=0, keepdims=True), (HALF, W)
        )
        return carry

    lax.fori_loop(0, chips, local_lags, 0)
    wait_bytes(par.at[pl.ds(0, chips - 1)], par_sem.at[1])

    def get_rate(b):
        rows = par[b].astype(f32)
        return rows, rows[:8] + rows[8:16]

    def mode_sums(i, carry):
        b = after(i)
        rate = get_rate(b)[1]
        far = jnp.exp(-float(W) * rate)
        parts = [rev[0, b], rev[1, b], sig[0, 1, b], sig[1, 1, b], lags[0, b], lags[1, b]]
        for chunk in range(2):
            parts.append((parts[2 + chunk].astype(f32) * (lane + 1.0)).astype(bf16))
            parts.append((parts[chunk].astype(f32) * lane).astype(bf16))
        found = [[] for _ in parts]
        for g in range(HALF):
            e = powers(rate[g : g + 1])
            rows = slice(16 * g, 16 * g + 16)
            res = dot(jnp.concatenate([part[rows] for part in parts], axis=0), e)
            for n in range(len(parts)):
                found[n].append(diag_row(mask, res[16 * n : 16 * n + 16]))
        found = [jnp.concatenate(rows, axis=0) for rows in found]
        for n in range(len(parts)):
            keep[b, n] = found[n]
        st = jnp.concatenate([found[0] * far + found[1], found[2] + far * found[3]], axis=0)
        st_out[b] = st.astype(bf16)

        @pl.when(i < chips)
        def _():
            remote(st_out.at[b], came.at[chip], st_sem, peer(b)).start()

        return carry

    lax.fori_loop(1, chips + 1, mode_sums, 0)
    came[chip] = st_out[chip]
    wait_bytes(came.at[pl.ds(0, chips - 1)], st_sem.at[1])

    decay2 = jnp.exp(-2.0 * float(W) * own_rate[...])

    def ahead(p, s):
        hold[p] = s
        return s * decay2 + came[p].astype(f32)[:HALF]

    lax.fori_loop(0, chips, ahead, jnp.zeros((HALF, LANES), f32))

    def back(i, s):
        p = chips - 1 - i
        ready[p] = jnp.concatenate([hold[p], s], axis=0).astype(bf16)
        return s * decay2 + came[p].astype(f32)[HALF:]

    lax.fori_loop(0, chips, back, jnp.zeros((HALF, LANES), f32))

    def send_back(i, carry):
        b = after(i)
        remote(ready.at[b], got.at[chip], back_sem, peer(b)).start()
        return carry

    lax.fori_loop(1, chips, send_back, 0)
    got[chip] = ready[chip]
    wait_bytes(got.at[pl.ds(0, chips - 1)], back_sem.at[1])

    def finish(i, carry):
        b = after(i)
        rows, rate = get_rate(b)
        weight = rows[16:24]
        bias_row = rows[24:25, :W] + rows[25:26, :W]
        state = got[b].astype(f32)
        near_decay = jnp.exp(-rate)
        far = jnp.exp(-float(W) * rate)
        s0, r1 = state[:HALF], state[HALF:]
        s1 = far * s0 + keep[b, 0]
        r0 = far * r1 + keep[b, 3]
        grad_a = keep[b, 4] + near_decay * (keep[b, 2] * s0 + keep[b, 3] * s1)
        grad_d = keep[b, 5] + near_decay * (
            float(W) * far * (s0 * r0 + s1 * r1)
            + s0 * keep[b, 6] + r0 * keep[b, 7] + s1 * keep[b, 8] + r1 * keep[b, 9]
        )
        skip_part = jnp.concatenate([skip[b], jnp.zeros((HALF, W), f32)], axis=1)
        grad_out[b] = jnp.concatenate([grad_a, grad_d, skip_part, skip_part], axis=0).astype(bf16)

        @pl.when(i < chips)
        def _():
            remote(grad_out.at[b], grad_in.at[chip], grad_sem, peer(b)).start()

        wa = weight * near_decay
        terms = [weight, wa * s0, wa * s1, wa * r0, wa * r1]
        for g in range(HALF):
            e = powers(rate[g : g + 1])
            lhs = jnp.concatenate(
                [jnp.where(mask, term[g : g + 1], 0.0) for term in terms], axis=0
            ).astype(bf16)
            z = dot_nt(lhs, e)
            for n in range(len(terms)):
                expand[n, 16 * g : 16 * g + 16] = z[16 * n : 16 * n + 16]
        x = jnp.concatenate([sig[0, 0, b], sig[1, 0, b]], axis=0)
        m = jnp.concatenate([sig[0, 1, b], sig[1, 1, b]], axis=0)
        spec_h = dot(expand[0].astype(bf16), fwd_ref[...])
        spec_h = jnp.concatenate([spec_h, spec_h], axis=0)
        gain = jnp.sum(jnp.where(eye, bias_row, 0.0), axis=1, keepdims=True)
        gain = jnp.concatenate([gain, gain], axis=0)
        y = dot(cmul(dot(x, fwd_ref[...]), spec_h), inv_ref[...])
        y += jnp.concatenate([expand[1], expand[2]], axis=0) + gain * x.astype(f32)
        p = dot(cmul(dot(m, fwdr_ref[...]), spec_h), invr_ref[...])
        p += dot(
            jnp.concatenate([expand[3], expand[4]], axis=0).astype(bf16), flip_ref[...]
        ) + gain * m.astype(f32)
        y, p = y.astype(bf16), p.astype(bf16)
        for chunk in range(2):
            stage[chunk, 0, b] = y[W * chunk : W * chunk + W]
            stage[chunk, 1, b] = p[W * chunk : W * chunk + W]
        for n, out in enumerate((mixed_hbm, pgrad_hbm)):
            pltpu.make_async_copy(stage.at[core, n, b], out.at[b, core], out_sem.at[2]).start()
            remote(stage.at[1 - core, n, b], out.at[b, core], out_sem, near).start()
        return carry

    lax.fori_loop(1, chips + 1, finish, 0)

    grad_in[chip] = grad_out[chip]
    wait_bytes(grad_in.at[pl.ds(0, chips - 1)], grad_sem.at[1])
    mine[...] = lax.fori_loop(
        0, chips, lambda p, s: s + grad_in[p].astype(f32), jnp.zeros(grad_in.shape[1:], f32)
    )
    swap = remote(mine, theirs, twin_sem, twin)
    swap.start()
    wait_bytes(own_many(par, chips), par_sem.at[0])
    wait_bytes(own_many(st_out, chips), st_sem.at[0])
    wait_bytes(own_many(ready, chips), back_sem.at[0])
    wait_bytes(own_many(grad_out, chips), grad_sem.at[0])
    for n in range(3):
        wait_bytes(stage.at[0], out_sem.at[n])
    swap.wait()
    total_ref[...] = mine[...] + theirs[...]


def own_many(ref, chips):
    return ref.at[pl.ds(0, chips - 1)]


def body(query, key_in, value_in, cotangent, residue, log_rate, bias):
    shards = lax.axis_size("ctx")
    channels, width = query.shape
    fwd, fwdr, inv, invr, flip = tables()
    rate = jnp.exp(log_rate)
    root = jnp.sqrt(-jnp.expm1(-2.0 * rate))
    rate_rows = rate.reshape(HALF, LANES)
    weight_rows = (residue * root).reshape(HALF, LANES)
    bias_row = jnp.pad(bias.reshape(1, W), ((0, 0), (0, LANES - W)))
    upper = lambda z: lax.reduce_precision(z, 8, 7)
    own_par = jnp.concatenate(
        [
            rate_rows,
            rate_rows - upper(rate_rows),
            weight_rows,
            bias_row,
            bias_row - upper(bias_row),
            jnp.zeros((6, LANES), f32),
        ],
        axis=0,
    ).astype(bf16)
    vmem = pl.BlockSpec(memory_space=pltpu.VMEM)
    dma = pltpu.SemaphoreType.DMA

    def remote(number):
        return pltpu.CompilerParams(
            collective_id=number, has_side_effects=True, vmem_limit_bytes=52 * 1024 * 1024
        )

    chips = shards // 2
    split = lambda z: z.reshape(chips, 2, W, width)
    anywhere = pl.BlockSpec(memory_space=pl.ANY)
    part = jax.ShapeDtypeStruct((chips, 2, W, width), bf16)
    mixed, pgrad, total = pl.pallas_call(
        mixer_kernel,
        in_specs=[anywhere] * 4 + [vmem] * 7,
        out_specs=[anywhere, anywhere, vmem],
        out_shape=[part, part, jax.ShapeDtypeStruct((32, LANES), f32)],
        scratch_shapes=[
            pltpu.VMEM((2, 4, chips, W, W), bf16),
            pltpu.VMEM((2, chips, W, W), bf16),
            pltpu.VMEM((2, 2, chips, W, W), bf16),
            pltpu.VMEM((2, chips, W, W), bf16),
            pltpu.VMEM((2, chips, W, W), bf16),
            pltpu.VMEM((chips, HALF, W), f32),
            pltpu.VMEM((chips, 32, LANES), bf16),
            pltpu.VMEM((chips, 10, HALF, LANES), f32),
            pltpu.VMEM((chips, 16, LANES), bf16),
            pltpu.VMEM((chips, 16, LANES), bf16),
            pltpu.VMEM((chips, HALF, LANES), f32),
            pltpu.VMEM((chips, 16, LANES), bf16),
            pltpu.VMEM((chips, 16, LANES), bf16),
            pltpu.VMEM((chips, 32, LANES), bf16),
            pltpu.VMEM((chips, 32, LANES), bf16),
            pltpu.VMEM((32, LANES), f32),
            pltpu.VMEM((32, LANES), f32),
            pltpu.VMEM((5, W, W), f32),
            pltpu.VMEM((2, 2, chips, W, W), bf16),
            dma((2,)),
            dma((2,)),
            dma((2,)),
            dma((2,)),
            dma((2,)),
            dma((2,)),
            dma((3,)),
            dma((2,)),
        ],
        compiler_params=remote(1),
        name="mixer",
    )(split(query), split(key_in), split(value_in), split(cotangent), own_par, rate_rows,
      fwd, fwdr, inv, invr, flip)
    mixed = mixed.reshape(channels, width)
    pgrad = pgrad.reshape(channels, width)
    gated, gq = mul16(query, mixed), mul16(cotangent, mixed)
    gk, gv = mul16(pgrad, value_in), mul16(pgrad, key_in)

    modes = residue.shape[1]
    grad_a = total[:HALF].reshape(-1, modes)
    grad_d = total[HALF:16].reshape(-1, modes)
    scale = 1.0 / math.sqrt(float(shards * width * lax.axis_size("dp")))
    grad_residue = root * grad_a * scale
    grad_rate = rate * residue * (jnp.exp(-2.0 * rate) / root * grad_a - root * grad_d) * scale
    grad_bias = total[16, :W] * scale
    return gated, gq, gk, gv, grad_residue, grad_rate, grad_bias


def solution(mesh):
    tok = P(None, ("dp", "ctx"))
    chan = P("ctx", None)
    return jax.shard_map(
        body,
        mesh=mesh,
        in_specs=(tok, tok, tok, tok, chan, chan, P("ctx")),
        out_specs=(tok, tok, tok, tok, chan, chan, P("ctx")),
        check_vma=False,
    )
```

```python
import functools
import math

import jax
import jax.numpy as jnp
import numpy as np
from jax import lax
from jax.experimental import pallas as pl
from jax.experimental.pallas import tpu as pltpu
from jax.sharding import PartitionSpec as P

bf16 = jnp.bfloat16
f32 = jnp.float32
W = 128
HALF = 8
MESH = pl.DeviceIdType.MESH
LANES = 256


def tables():
    n = np.arange(W)[:, None]
    f = np.arange(W)[None, :]
    angle = ((2 * f + 1) * n % (4 * W)) * (2.0 * math.pi / (4 * W))
    fwd = np.concatenate([np.cos(angle), -np.sin(angle)], axis=1)
    inv = fwd.T / W
    flip = np.eye(W)[::-1]
    pad = np.concatenate([flip, np.zeros((W, W))], axis=1)
    packed = np.concatenate([fwd, fwd[::-1], np.concatenate([inv, inv[:, ::-1]], axis=1), pad])
    return jnp.asarray(packed, f32).astype(bf16)


def dot(a, b):
    return jnp.dot(a, b, preferred_element_type=f32)


def dot_nt(a, b):
    return lax.dot_general(a, b, (((1,), (1,)), ((), ())), preferred_element_type=f32)


def powers(rate_row):
    rate8 = jnp.broadcast_to(rate_row, (8, LANES))
    row = lax.broadcasted_iota(jnp.int32, (8, LANES), 0).astype(f32)
    out = jnp.exp(-rate8 * row)
    for step in (8, 16, 32, 64):
        mult = jnp.exp(-rate8 * float(step))
        parts = [out[i : i + 8] * mult for i in range(0, step, 8)]
        out = jnp.concatenate([out] + parts, axis=0)
    return out.astype(bf16)


def diag_mask():
    row = lax.broadcasted_iota(jnp.int32, (16, LANES), 0)
    lane = lax.broadcasted_iota(jnp.int32, (16, LANES), 1)
    return row == lane // 16


def diag_row(mask, rows):
    return jnp.sum(jnp.where(mask, rows, 0.0), axis=0, keepdims=True)


def mul16(a, b):
    return (a.astype(f32) * b.astype(f32)).astype(bf16)


def cmul(a, b):
    ar, ai, br, bi = a[:, :W], a[:, W:], b[:, :W], b[:, W:]
    return jnp.concatenate([ar * br - ai * bi, ar * bi + ai * br], axis=1).astype(bf16)


def wait_bytes(ref, sem):
    pltpu.make_async_copy(ref, ref, sem).wait()


def mixer_kernel(
    q_hbm, k_hbm, v_hbm, c_hbm, tab_hbm, own_ref, mixed_hbm, pgrad_hbm, total_ref, tab, inp, away, sig, rev, lags, skip, par, keep, st_out, came, hold, ready, got, grad_out,
    grad_in, mine, theirs, stage,
    load_sem, par_sem, pair_sem, st_sem, back_sem, grad_sem, out_sem, twin_sem,
):
    chips = q_hbm.shape[0]
    me = lax.axis_index("ctx")
    core, chip = lax.rem(me, 2), lax.div(me, 2)
    near = {"ctx": me + 1 - 2 * core}
    twin = {"dp": 1 - lax.axis_index("dp")}

    def peer(b):
        return {"ctx": 2 * b + core}

    def after(i):
        return lax.rem(chip + i, chips)

    def remote(src, dst, sems, who):
        return pltpu.make_async_remote_copy(
            src_ref=src, dst_ref=dst, send_sem=sems.at[0], recv_sem=sems.at[1],
            device_id=who, device_id_type=MESH,
        )

    for order in range(2):
        side = 1 - core if order == 0 else core
        for n, ref in enumerate((q_hbm, k_hbm, v_hbm, c_hbm)):
            pltpu.make_async_copy(ref.at[:, side], inp.at[order, n], load_sem.at[order]).start()

    pltpu.make_async_copy(tab_hbm, tab, load_sem.at[2]).start()
    fwd_ref, fwdr_ref = tab.at[0:W], tab.at[W : 2 * W]
    inv_ref, invr_ref = tab.at[2 * W : 4 * W, 0:W], tab.at[2 * W : 4 * W, W : 2 * W]
    flip_ref = tab.at[4 * W : 5 * W, 0:W]
    own = own_ref[...]
    low = own - own.astype(bf16).astype(f32)
    par[chip] = jnp.concatenate([own[:8], low[:8], own[8:16], own[16:17], low[16:17], own[18:24]], axis=0).astype(bf16)

    barrier = pltpu.get_barrier_semaphore()

    def tell(i, carry):
        pl.semaphore_signal(barrier, inc=1, device_id=peer(after(i)), device_id_type=MESH)
        return carry

    lax.fori_loop(1, chips, tell, 0)
    pl.semaphore_signal(barrier, inc=1, device_id=near, device_id_type=MESH)
    pl.semaphore_signal(barrier, inc=1, device_id=twin, device_id_type=MESH)
    pl.semaphore_wait(barrier, chips + 1)

    def send_par(i, carry):
        remote(par.at[chip], par.at[chip], par_sem, peer(after(i))).start()
        return carry

    lax.fori_loop(1, chips, send_par, 0)

    pieces = 4
    count = chips // pieces

    def products(order, dst, first):
        def step(i, carry):
            for b in (first + 2 * i, first + 2 * i + 1):
                dst[0, b] = mul16(inp[order, 1, b], inp[order, 2, b])
                dst[1, b] = mul16(inp[order, 3, b], inp[order, 0, b])
            return carry

        lax.fori_loop(0, count // 2, step, 0)

    wait_bytes(inp.at[0], load_sem.at[0])
    for n in range(pieces):
        products(0, away, n * count)
        block = pl.ds(n * count, count)
        pltpu.make_async_remote_copy(
            src_ref=away.at[:, block], dst_ref=sig.at[core, :, block], send_sem=pair_sem.at[pieces],
            recv_sem=pair_sem.at[n], device_id=near, device_id_type=MESH,
        ).start()
    wait_bytes(inp.at[1], load_sem.at[1])
    for n in range(pieces):
        products(1, sig.at[core], n * count)
    wait_bytes(tab, load_sem.at[2])

    eye = lax.broadcasted_iota(jnp.int32, (W, W), 0) == lax.broadcasted_iota(jnp.int32, (W, W), 1)
    lane = lax.broadcasted_iota(jnp.int32, (W, W), 1).astype(f32)
    mask = diag_mask()

    def local_lags(first, some):
        blocks = [first + n for n in range(some)]
        xs = [jnp.concatenate([sig[0, 0, b], sig[1, 0, b]], axis=0) for b in blocks]
        ms = [jnp.concatenate([sig[0, 1, b], sig[1, 1, b]], axis=0) for b in blocks]
        spec_x = [dot(x, fwd_ref[...]) for x in xs]
        spec_m = [dot(m, fwdr_ref[...]) for m in ms]
        turned = [dot(x, flip_ref[...]).astype(bf16) for x in xs]
        found = [dot(cmul(a, b), invr_ref[...]) for a, b in zip(spec_x, spec_m)]
        for n, b in enumerate(blocks):
            rev[0, b] = turned[n][:W]
            rev[1, b] = turned[n][W:]
            lag = found[n][:W] + found[n][W:]
            lags[0, b] = lag.astype(bf16)
            lags[1, b] = (lag * lane).astype(bf16)
            xm = xs[n].astype(f32) * ms[n].astype(f32)
            sums = jnp.sum(xm[:W] + xm[W:], axis=1, keepdims=True)
            skip[b] = jnp.broadcast_to(
                jnp.sum(jnp.where(eye, sums, 0.0), axis=0, keepdims=True), (HALF, W)
            )

    for n in range(pieces):
        block = pl.ds(n * count, count)
        wait_bytes(sig.at[core, :, block], pair_sem.at[n])

        def step(i, carry, n=n):
            local_lags(n * count + 4 * i, 4)
            return carry

        lax.fori_loop(0, count // 4, step, 0)
    wait_bytes(par.at[pl.ds(0, chips - 1)], par_sem.at[1])

    def get_rate(b):
        rows = par[b].astype(f32)
        return rows, rows[:8] + rows[8:16]

    def mode_sums(b):
        rate = get_rate(b)[1]
        far = jnp.exp(-float(W) * rate)
        parts = [rev[0, b], rev[1, b], sig[0, 1, b], sig[1, 1, b], lags[0, b], lags[1, b]]
        for chunk in range(2):
            parts.append((parts[2 + chunk].astype(f32) * (lane + 1.0)).astype(bf16))
            parts.append((parts[chunk].astype(f32) * lane).astype(bf16))
        found = [[] for _ in parts]
        for g in range(HALF):
            e = powers(rate[g : g + 1])
            rows = slice(16 * g, 16 * g + 16)
            res = dot(jnp.concatenate([part[rows] for part in parts], axis=0), e)
            for n in range(len(parts)):
                found[n].append(diag_row(mask, res[16 * n : 16 * n + 16]))
        found = [jnp.concatenate(rows, axis=0) for rows in found]
        st = jnp.concatenate([found[0] * far + found[1], found[2] + far * found[3]], axis=0)
        return found, st.astype(bf16)

    def sum_step(i, carry):
        blocks = [after(2 * i + 1), after(2 * i + 2)]
        results = [mode_sums(b) for b in blocks]
        for b, (found, st) in zip(blocks, results):
            for n, value in enumerate(found):
                keep[b, n] = value
            st_out[b] = st
        remote(st_out.at[blocks[0]], came.at[chip], st_sem, peer(blocks[0])).start()

        @pl.when(2 * i + 2 < chips)
        def _():
            remote(st_out.at[blocks[1]], came.at[chip], st_sem, peer(blocks[1])).start()

        return carry

    lax.fori_loop(0, chips // 2, sum_step, 0)
    came[chip] = st_out[chip]
    wait_bytes(came.at[pl.ds(0, chips - 1)], st_sem.at[1])

    decay2 = jnp.exp(-2.0 * float(W) * own[:8])

    def ahead(p, s):
        hold[p] = s
        return s * decay2 + came[p].astype(f32)[:HALF]

    lax.fori_loop(0, chips, ahead, jnp.zeros((HALF, LANES), f32))

    def back(i, s):
        p = chips - 1 - i
        ready[p] = jnp.concatenate([hold[p], s], axis=0).astype(bf16)
        return s * decay2 + came[p].astype(f32)[HALF:]

    lax.fori_loop(0, chips, back, jnp.zeros((HALF, LANES), f32))

    def send_back(i, carry):
        b = after(i)
        remote(ready.at[b], got.at[chip], back_sem, peer(b)).start()
        return carry

    lax.fori_loop(1, chips, send_back, 0)
    got[chip] = ready[chip]
    wait_bytes(got.at[pl.ds(0, chips - 1)], back_sem.at[1])

    def chunk_states(b, rate):
        state = got[b].astype(f32)
        far = jnp.exp(-float(W) * rate)
        s0, r1 = state[:HALF], state[HALF:]
        return s0, far * s0 + keep[b, 0], far * r1 + keep[b, 3], r1

    def send_grads(i, carry):
        b = after(i)
        rate = get_rate(b)[1]
        near_decay = jnp.exp(-rate)
        s0, s1, r0, r1 = chunk_states(b, rate)
        grad_a = keep[b, 4] + near_decay * (keep[b, 2] * s0 + keep[b, 3] * s1)
        grad_d = keep[b, 5] + near_decay * (
            float(W) * jnp.exp(-float(W) * rate) * (s0 * r0 + s1 * r1)
            + s0 * keep[b, 6] + r0 * keep[b, 7] + s1 * keep[b, 8] + r1 * keep[b, 9]
        )
        skip_part = jnp.concatenate([skip[b], jnp.zeros((HALF, W), f32)], axis=1)
        grad_out[b] = jnp.concatenate([grad_a, grad_d, skip_part, skip_part], axis=0).astype(bf16)

        @pl.when(i < chips)
        def _():
            remote(grad_out.at[b], grad_in.at[chip], grad_sem, peer(b)).start()

        return carry

    lax.fori_loop(1, chips + 1, send_grads, 0)
    grad_in[chip] = grad_out[chip]

    def expand(b):
        rows, rate = get_rate(b)
        s0, s1, r0, r1 = chunk_states(b, rate)
        wa = rows[16:24] * jnp.exp(-rate)
        terms = [rows[16:24], wa * s0, wa * s1, wa * r0, wa * r1]
        made = []
        for g in range(HALF):
            e = powers(rate[g : g + 1])
            lhs = jnp.concatenate(
                [jnp.where(mask, term[g : g + 1], 0.0) for term in terms], axis=0
            ).astype(bf16)
            made.append(dot_nt(lhs, e))
        return [jnp.concatenate([z[16 * n : 16 * n + 16] for z in made], axis=0) for n in range(5)]

    def convolve(b, taps, y0, y1, p0, p1):
        rows = par[b].astype(f32)
        bias_row = rows[24:25, :W] + rows[25:26, :W]
        x = jnp.concatenate([sig[0, 0, b], sig[1, 0, b]], axis=0)
        m = jnp.concatenate([sig[0, 1, b], sig[1, 1, b]], axis=0)
        spec_x, spec_m = dot(x, fwd_ref[...]), dot(m, fwdr_ref[...])
        spec_h = dot(taps.astype(bf16), fwd_ref[...])
        spec_h = jnp.concatenate([spec_h, spec_h], axis=0)
        gain = jnp.sum(jnp.where(eye, bias_row, 0.0), axis=1, keepdims=True)
        gain = jnp.concatenate([gain, gain], axis=0)
        y = dot(cmul(spec_x, spec_h), inv_ref[...])
        y += jnp.concatenate([y0, y1], axis=0) + gain * x.astype(f32)
        p = dot(cmul(spec_m, spec_h), invr_ref[...])
        p += dot(jnp.concatenate([p0, p1], axis=0).astype(bf16), flip_ref[...])
        p += gain * m.astype(f32)
        return y.astype(bf16), p.astype(bf16)

    def finish(i, carry):
        blocks = [after(2 * i + 1), after(2 * i + 2)]
        grown = [expand(b) for b in blocks]
        results = [convolve(b, *terms) for b, terms in zip(blocks, grown)]
        for b, result in zip(blocks, results):
            for chunk in range(2):
                for n in range(2):
                    stage[chunk, n, b] = result[n][W * chunk : W * chunk + W]
        for b in blocks:
            for n, out in enumerate((mixed_hbm, pgrad_hbm)):
                pltpu.make_async_copy(stage.at[core, n, b], out.at[b, core], out_sem.at[2]).start()
                remote(stage.at[1 - core, n, b], out.at[b, core], out_sem, near).start()
        return carry

    early = 3 * chips // 8
    lax.fori_loop(0, early, finish, 0)
    wait_bytes(grad_in.at[pl.ds(0, chips - 1)], grad_sem.at[1])
    mine[...] = lax.fori_loop(
        0, chips, lambda p, s: s + grad_in[p].astype(f32), jnp.zeros(grad_in.shape[1:], f32)
    )
    swap = remote(mine, theirs, twin_sem, twin)
    swap.start()
    lax.fori_loop(early, chips // 2, finish, 0)
    wait_bytes(away, pair_sem.at[pieces])
    wait_bytes(own_many(par, chips), par_sem.at[0])
    wait_bytes(own_many(st_out, chips), st_sem.at[0])
    wait_bytes(own_many(ready, chips), back_sem.at[0])
    wait_bytes(own_many(grad_out, chips), grad_sem.at[0])
    for n in range(3):
        wait_bytes(stage.at[0], out_sem.at[n])
    swap.wait()
    total_ref[...] = mine[...] + theirs[...]


def own_many(ref, chips):
    return ref.at[pl.ds(0, chips - 1)]


def body(query, key_in, value_in, cotangent, residue, log_rate, bias):
    shards = lax.axis_size("ctx")
    channels, width = query.shape
    rate = jnp.exp(log_rate)
    root = jnp.sqrt(-jnp.expm1(-2.0 * rate))
    own = jnp.concatenate(
        [
            rate.reshape(HALF, LANES),
            (residue * root).reshape(HALF, LANES),
            jnp.pad(bias.reshape(1, W), ((0, 7), (0, LANES - W))),
        ],
        axis=0,
    )
    vmem = pl.BlockSpec(memory_space=pltpu.VMEM)
    dma = pltpu.SemaphoreType.DMA

    def remote(number):
        return pltpu.CompilerParams(
            collective_id=number, has_side_effects=True, vmem_limit_bytes=52 * 1024 * 1024
        )

    chips = shards // 2
    split = lambda z: z.reshape(chips, 2, W, width)
    anywhere = pl.BlockSpec(memory_space=pl.ANY)
    part = jax.ShapeDtypeStruct((chips, 2, W, width), bf16)
    mixed, pgrad, total = pl.pallas_call(
        mixer_kernel,
        in_specs=[anywhere] * 5 + [vmem],
        out_specs=[anywhere, anywhere, vmem],
        out_shape=[part, part, jax.ShapeDtypeStruct((32, LANES), f32)],
        scratch_shapes=[
            pltpu.VMEM((5 * W, LANES), bf16),
            pltpu.VMEM((2, 4, chips, W, W), bf16),
            pltpu.VMEM((2, chips, W, W), bf16),
            pltpu.VMEM((2, 2, chips, W, W), bf16),
            pltpu.VMEM((2, chips, W, W), bf16),
            pltpu.VMEM((2, chips, W, W), bf16),
            pltpu.VMEM((chips, HALF, W), f32),
            pltpu.VMEM((chips, 32, LANES), bf16),
            pltpu.VMEM((chips, 10, HALF, LANES), f32),
            pltpu.VMEM((chips, 16, LANES), bf16),
            pltpu.VMEM((chips, 16, LANES), bf16),
            pltpu.VMEM((chips, HALF, LANES), f32),
            pltpu.VMEM((chips, 16, LANES), bf16),
            pltpu.VMEM((chips, 16, LANES), bf16),
            pltpu.VMEM((chips, 32, LANES), bf16),
            pltpu.VMEM((chips, 32, LANES), bf16),
            pltpu.VMEM((32, LANES), f32),
            pltpu.VMEM((32, LANES), f32),
            pltpu.VMEM((2, 2, chips, W, W), bf16),
            dma((3,)),
            dma((2,)),
            dma((5,)),
            dma((2,)),
            dma((2,)),
            dma((2,)),
            dma((3,)),
            dma((2,)),
        ],
        compiler_params=remote(1),
        name="mixer",
    )(split(query), split(key_in), split(value_in), split(cotangent), tables(), own)
    mixed = mixed.reshape(channels, width)
    pgrad = pgrad.reshape(channels, width)
    gated, gq = mul16(query, mixed), mul16(cotangent, mixed)
    gk, gv = mul16(pgrad, value_in), mul16(pgrad, key_in)

    modes = residue.shape[1]
    grad_a = total[:HALF].reshape(-1, modes)
    grad_d = total[HALF:16].reshape(-1, modes)
    scale = 1.0 / math.sqrt(float(shards * width * lax.axis_size("dp")))
    grad_residue = root * grad_a * scale
    grad_rate = rate * residue * (jnp.exp(-2.0 * rate) / root * grad_a - root * grad_d) * scale
    grad_bias = total[16, :W] * scale
    return gated, gq, gk, gv, grad_residue, grad_rate, grad_bias


def solution(mesh):
    tok = P(None, ("dp", "ctx"))
    chan = P("ctx", None)
    return jax.shard_map(
        body,
        mesh=mesh,
        in_specs=(tok, tok, tok, tok, chan, chan, P("ctx")),
        out_specs=(tok, tok, tok, tok, chan, chan, P("ctx")),
        check_vma=False,
    )
```

```python
import functools
import math

import jax
import jax.numpy as jnp
import numpy as np
from jax import lax
from jax.experimental import pallas as pl
from jax.experimental.pallas import tpu as pltpu
from jax.sharding import PartitionSpec as P

bf16 = jnp.bfloat16
f32 = jnp.float32
W = 128
HALF = 8
MESH = pl.DeviceIdType.MESH
LANES = 256


def tables():
    n = np.arange(W)[:, None]
    f = np.arange(W)[None, :]
    angle = ((2 * f + 1) * n % (4 * W)) * (2.0 * math.pi / (4 * W))
    fwd = np.concatenate([np.cos(angle), -np.sin(angle)], axis=1)
    inv = fwd.T / W
    flip = np.eye(W)[::-1]
    pad = np.concatenate([flip, np.zeros((W, W))], axis=1)
    packed = np.concatenate([fwd, fwd[::-1], np.concatenate([inv, inv[:, ::-1]], axis=1), pad])
    return jnp.asarray(packed, f32)


def dot(a, b):
    return jnp.dot(a, b, preferred_element_type=f32)


def dot_nt(a, b):
    return lax.dot_general(a, b, (((1,), (1,)), ((), ())), preferred_element_type=f32)


def powers(rate_row):
    rate8 = jnp.broadcast_to(rate_row, (8, LANES))
    row = lax.broadcasted_iota(jnp.int32, (8, LANES), 0).astype(f32)
    out = jnp.exp(-rate8 * row)
    for step in (8, 16, 32, 64):
        mult = jnp.exp(-rate8 * float(step))
        parts = [out[i : i + 8] * mult for i in range(0, step, 8)]
        out = jnp.concatenate([out] + parts, axis=0)
    return out.astype(bf16)


def diag_mask():
    row = lax.broadcasted_iota(jnp.int32, (16, LANES), 0)
    lane = lax.broadcasted_iota(jnp.int32, (16, LANES), 1)
    return row == lane // 16


def diag_row(mask, rows):
    return jnp.sum(jnp.where(mask, rows, 0.0), axis=0, keepdims=True)


def mul16(a, b):
    return (a.astype(f32) * b.astype(f32)).astype(bf16)


def cmul(a, b):
    ar, ai, br, bi = a[:, :W], a[:, W:], b[:, :W], b[:, W:]
    return jnp.concatenate([ar * br - ai * bi, ar * bi + ai * br], axis=1).astype(bf16)


def wait_bytes(ref, sem):
    pltpu.make_async_copy(ref, ref, sem).wait()


def mixer_kernel(
    q_hbm, k_hbm, v_hbm, c_hbm, tab_hbm, own_ref, mixed_hbm, pgrad_hbm, total_ref,
    tab32, tab, inp, away, sig, rev, lags, skip, par, keep, st_out, came, hold, ready, got,
    grad_out, grad_in, mine, theirs, stage,
    load_sem, par_sem, pair_sem, st_sem, back_sem, grad_sem, out_sem, twin_sem,
):
    pairs = q_hbm.shape[0]
    chips = 2 * pairs
    steps = pairs // 2
    quad = HALF // 2
    me = lax.axis_index("ctx")
    core, chip = lax.rem(me, 2), lax.div(me, 2)
    near = {"ctx": me + 1 - 2 * core}
    twin = {"dp": 1 - lax.axis_index("dp")}

    def peer(b):
        return {"ctx": 2 * b + core}

    def after(i):
        return lax.rem(chip + i, chips)

    def remote(src, dst, send, recv, who):
        return pltpu.make_async_remote_copy(
            src_ref=src, dst_ref=dst, send_sem=send, recv_sem=recv,
            device_id=who, device_id_type=MESH,
        )

    for order in range(2):
        side = 1 - core if order == 0 else core
        for half in range(2):
            for n, ref in enumerate((q_hbm, k_hbm, v_hbm, c_hbm)):
                pltpu.make_async_copy(
                    ref.at[:, :, side, half], inp.at[order, n, pl.ds(half * pairs, pairs)],
                    load_sem.at[order],
                ).start()
    pltpu.make_async_copy(tab_hbm, tab32, load_sem.at[2]).start()

    barrier = pltpu.get_barrier_semaphore()

    def tell(i, carry):
        pl.semaphore_signal(barrier, inc=1, device_id=peer(after(i)), device_id_type=MESH)
        return carry

    lax.fori_loop(1, chips, tell, 0)
    pl.semaphore_signal(barrier, inc=1, device_id=near, device_id_type=MESH)
    pl.semaphore_signal(barrier, inc=1, device_id=twin, device_id_type=MESH)

    own = own_ref[...]
    low = own - own.astype(bf16).astype(f32)
    for half in range(2):
        rows = slice(quad * half, quad * half + quad)
        par[chip, half] = jnp.concatenate(
            [
                own[:8][rows],
                low[:8][rows],
                own[8:16][rows],
                own[16 + half : 17 + half],
                low[16 + half : 17 + half],
                own[17 - half : 18 - half],
                low[17 - half : 18 - half],
            ],
            axis=0,
        ).astype(bf16)

    fwd_ref, fwdr_ref = tab.at[0:W], tab.at[W : 2 * W]
    inv_ref, invr_ref = tab.at[2 * W : 4 * W, 0:W], tab.at[2 * W : 4 * W, W : 2 * W]
    flip_ref = tab.at[4 * W : 5 * W, 0:W]

    pieces = 4
    count = chips // pieces

    def products(order, dst, first):
        def step(i, carry):
            for v in (first + 2 * i, first + 2 * i + 1):
                dst[0, v] = mul16(inp[order, 1, v], inp[order, 2, v]).reshape(W, W)
                dst[1, v] = mul16(inp[order, 3, v], inp[order, 0, v]).reshape(W, W)
            return carry

        lax.fori_loop(0, count // 2, step, 0)

    def send_par(i, carry):
        remote(
            par.at[chip], par.at[chip], par_sem.at[0], par_sem.at[1], peer(after(i))
        ).start()
        return carry

    wait_bytes(inp.at[0], load_sem.at[0])
    for n in range(pieces):
        products(0, away, n * count)
        if n == 0:
            pl.semaphore_wait(barrier, chips + 1)
            lax.fori_loop(1, chips, send_par, 0)
        block = pl.ds(n * count, count)
        remote(
            away.at[:, block], sig.at[core, :, block], pair_sem.at[pieces], pair_sem.at[n], near
        ).start()
    wait_bytes(inp.at[1], load_sem.at[1])
    for n in range(pieces):
        products(1, sig.at[core], n * count)
    wait_bytes(tab32, load_sem.at[2])
    tab[...] = tab32[...].astype(bf16)

    row_no = lax.broadcasted_iota(jnp.int32, (W, W), 0)
    lane_no = lax.broadcasted_iota(jnp.int32, (W, W), 1)
    eye = row_no == lane_no
    swapped_eye = lax.rem(row_no + W // 2, W) == lane_no
    lane = lax.broadcasted_iota(jnp.int32, (W, W), 1).astype(f32)
    mask = diag_mask()

    def local_lags(first, some):
        blocks = [first + n for n in range(some)]
        xs = [jnp.concatenate([sig[0, 0, v], sig[1, 0, v]], axis=0) for v in blocks]
        ms = [jnp.concatenate([sig[0, 1, v], sig[1, 1, v]], axis=0) for v in blocks]
        spec_x = [dot(x, fwd_ref[...]) for x in xs]
        spec_m = [dot(m, fwdr_ref[...]) for m in ms]
        turned = [dot(x, flip_ref[...]).astype(bf16) for x in xs]
        found = [dot(cmul(a, b), invr_ref[...]) for a, b in zip(spec_x, spec_m)]
        for n, v in enumerate(blocks):
            rev[0, v] = turned[n][:W]
            rev[1, v] = turned[n][W:]
            lag = found[n][:W] + found[n][W:]
            lags[0, v] = lag.astype(bf16)
            lags[1, v] = (lag * lane).astype(bf16)
            xm = xs[n].astype(f32) * ms[n].astype(f32)
            sums = jnp.sum(xm[:W] + xm[W:], axis=1, keepdims=True)
            for side, where in enumerate((eye, swapped_eye)):
                skip[v, HALF * side : HALF * side + HALF] = jnp.broadcast_to(
                    jnp.sum(jnp.where(where, sums, 0.0), axis=0, keepdims=True), (HALF, W)
                )

    for n in range(pieces):
        block = pl.ds(n * count, count)
        wait_bytes(sig.at[core, :, block], pair_sem.at[n])

        def step(i, carry, n=n):
            local_lags(n * count + 4 * i, 4)
            return carry

        lax.fori_loop(0, count // 4, step, 0)
    wait_bytes(par.at[pl.ds(0, chips - 1)], par_sem.at[1])

    def place(j, n):
        half = lax.div(j, steps)
        u = lax.rem(lax.div(chip, 2) + 2 * lax.rem(j, steps) + 1 + n, pairs)
        return half, u, half * pairs + u

    def halves(first, second, start):
        rows = slice(start, start + quad)
        return jnp.concatenate([first[rows], second[rows]], axis=0)

    def get_par(half, u):
        return par[2 * u, half].astype(f32), par[2 * u + 1, half].astype(f32)

    def get_rate(pair):
        return halves(*pair, 0) + halves(*pair, quad)

    def mode_sums(half, u, v):
        rate = get_rate(get_par(half, u))
        far = jnp.exp(-float(W) * rate)
        parts = [rev[0, v], rev[1, v], sig[0, 1, v], sig[1, 1, v], lags[0, v], lags[1, v]]
        for chunk in range(2):
            parts.append((parts[2 + chunk].astype(f32) * (lane + 1.0)).astype(bf16))
            parts.append((parts[chunk].astype(f32) * lane).astype(bf16))
        found = [[] for _ in parts]
        for g in range(HALF):
            e = powers(rate[g : g + 1])
            rows = slice(16 * g, 16 * g + 16)
            res = dot(jnp.concatenate([part[rows] for part in parts], axis=0), e)
            for n in range(len(parts)):
                found[n].append(diag_row(mask, res[16 * n : 16 * n + 16]))
        found = [jnp.concatenate(rows, axis=0) for rows in found]
        return found, found[0] * far + found[1], found[2] + far * found[3]

    def sum_step(j, carry):
        places = [place(j, n) for n in range(2)]
        results = [mode_sums(*where) for where in places]
        for (half, u, v), (found, ahead, back) in zip(places, results):
            for n, value in enumerate(found):
                keep[v, n] = value
            for n in range(2):
                rows = slice(quad * n, quad * n + quad)
                st_out[half, 2 * u + n] = jnp.concatenate([ahead[rows], back[rows]], axis=0)
        for half, u, v in places:
            for n in range(2):
                b = 2 * u + n

                @pl.when(b != chip)
                def _(b=b, half=half):
                    remote(
                        st_out.at[half, b], came.at[half, chip], st_sem.at[half, 0],
                        st_sem.at[half, 1], peer(b),
                    ).start()

        return carry

    def scan(half):
        came[half, chip] = st_out[half, chip]
        wait_bytes(came.at[half, pl.ds(0, chips - 1)], st_sem.at[half, 1])
        decay2 = jnp.exp(-2.0 * float(W) * own[quad * half : quad * half + quad])

        def ahead(p, s):
            hold[p, 0:quad] = s
            return s * decay2 + came[half, p][:quad]

        lax.fori_loop(0, chips, ahead, jnp.zeros((quad, LANES), f32))

        def back(i, s):
            p = chips - 1 - i
            ready[half, p] = jnp.concatenate([hold[p, 0:quad], s], axis=0)
            return s * decay2 + came[half, p][quad:]

        lax.fori_loop(0, chips, back, jnp.zeros((quad, LANES), f32))

        def send_back(i, carry):
            b = after(i)
            remote(
                ready.at[half, b], got.at[half, chip], back_sem.at[half, 0], back_sem.at[half, 1],
                peer(b),
            ).start()
            return carry

        lax.fori_loop(1, chips, send_back, 0)
        got[half, chip] = ready[half, chip]

    def chunk_states(half, u, v, rate):
        pair = got[half, 2 * u], got[half, 2 * u + 1]
        far = jnp.exp(-float(W) * rate)
        s0, r1 = halves(*pair, 0), halves(*pair, quad)
        return s0, far * s0 + keep[v, 0], far * r1 + keep[v, 3], r1

    def send_grads(half):
        wait_bytes(got.at[half, pl.ds(0, chips - 1)], back_sem.at[half, 1])

        def step(i, carry):
            u = lax.rem(lax.div(chip, 2) + 1 + i, pairs)
            v = half * pairs + u
            rate = get_rate(get_par(half, u))
            near_decay = jnp.exp(-rate)
            s0, s1, r0, r1 = chunk_states(half, u, v, rate)
            grad_a = keep[v, 4] + near_decay * (keep[v, 2] * s0 + keep[v, 3] * s1)
            grad_d = keep[v, 5] + near_decay * (
                float(W) * jnp.exp(-float(W) * rate) * (s0 * r0 + s1 * r1)
                + s0 * keep[v, 6] + r0 * keep[v, 7] + s1 * keep[v, 8] + r1 * keep[v, 9]
            )
            for n in range(2):
                rows = slice(quad * n, quad * n + quad)
                first = 0 if n == half else HALF
                skip_part = jnp.concatenate(
                    [skip[v, first : first + HALF], jnp.zeros((HALF, W), f32)], axis=1
                )
                grad_out[half, 2 * u + n] = jnp.concatenate(
                    [grad_a[rows], grad_d[rows], skip_part], axis=0
                ).astype(bf16)
            for n in range(2):
                b = 2 * u + n

                @pl.when(b != chip)
                def _(b=b):
                    remote(
                        grad_out.at[half, b], grad_in.at[half, chip], grad_sem.at[half, 0],
                        grad_sem.at[half, 1], peer(b),
                    ).start()

            return carry

        lax.fori_loop(0, pairs, step, 0)
        grad_in[half, chip] = grad_out[half, chip]

    def expand(half, u, v):
        pair = get_par(half, u)
        rate, weight = get_rate(pair), halves(*pair, 2 * quad)
        s0, s1, r0, r1 = chunk_states(half, u, v, rate)
        wa = weight * jnp.exp(-rate)
        terms = [weight, wa * s0, wa * s1, wa * r0, wa * r1]
        made = []
        for g in range(HALF):
            e = powers(rate[g : g + 1])
            lhs = jnp.concatenate(
                [jnp.where(mask, term[g : g + 1], 0.0) for term in terms], axis=0
            ).astype(bf16)
            made.append(dot_nt(lhs, e))
        return [jnp.concatenate([z[16 * n : 16 * n + 16] for z in made], axis=0) for n in range(5)]

    def convolve(half, u, v, taps, y0, y1, p0, p1):
        pair = get_par(half, u)
        even, odd = pair[0][12:13, :W] + pair[0][13:14, :W], pair[1][14:15, :W] + pair[1][15:, :W]
        bias_row = jnp.where(lane[:1] < W // 2, even, odd)
        x = jnp.concatenate([sig[0, 0, v], sig[1, 0, v]], axis=0)
        m = jnp.concatenate([sig[0, 1, v], sig[1, 1, v]], axis=0)
        spec_x, spec_m = dot(x, fwd_ref[...]), dot(m, fwdr_ref[...])
        spec_h = dot(taps.astype(bf16), fwd_ref[...])
        spec_h = jnp.concatenate([spec_h, spec_h], axis=0)
        gain = jnp.sum(jnp.where(eye, bias_row, 0.0), axis=1, keepdims=True)
        gain = jnp.concatenate([gain, gain], axis=0)
        y = dot(cmul(spec_x, spec_h), inv_ref[...])
        y += jnp.concatenate([y0, y1], axis=0) + gain * x.astype(f32)
        p = dot(cmul(spec_m, spec_h), invr_ref[...])
        p += dot(jnp.concatenate([p0, p1], axis=0).astype(bf16), flip_ref[...])
        p += gain * m.astype(f32)
        return y.astype(bf16), p.astype(bf16)

    def finish(j, carry):
        places = [place(j, n) for n in range(2)]
        grown = [expand(*where) for where in places]
        results = [convolve(*where, *terms) for where, terms in zip(places, grown)]
        for (half, u, v), result in zip(places, results):
            for chunk in range(2):
                for n in range(2):
                    stage[chunk, n, v] = result[n][W * chunk : W * chunk + W].reshape(2, W // 2, W)
        for half, u, v in places:
            for n, out in enumerate((mixed_hbm, pgrad_hbm)):
                spot = out.at[u, :, core, half]
                pltpu.make_async_copy(stage.at[core, n, v], spot, out_sem.at[2]).start()
                remote(stage.at[1 - core, n, v], spot, out_sem.at[0], out_sem.at[1], near).start()
        return carry

    middle = steps + 5 * steps // 8
    lax.fori_loop(0, middle, sum_step, 0)
    scan(0)
    lax.fori_loop(middle, 2 * steps, sum_step, 0)
    send_grads(0)
    lax.fori_loop(0, steps // 4, finish, 0)
    scan(1)
    lax.fori_loop(steps // 4, steps, finish, 0)
    send_grads(1)
    early = steps + 3 * steps // 4
    lax.fori_loop(steps, early, finish, 0)
    for half in range(2):
        wait_bytes(grad_in.at[half, pl.ds(0, chips - 1)], grad_sem.at[half, 1])
        mine[half] = lax.fori_loop(
            0, chips, lambda p, t: t + grad_in[half, p].astype(f32), jnp.zeros((16, LANES), f32)
        )
    swap = remote(mine, theirs, twin_sem.at[0], twin_sem.at[1], twin)
    swap.start()
    lax.fori_loop(early, 2 * steps, finish, 0)
    wait_bytes(away, pair_sem.at[pieces])
    wait_bytes(par.at[pl.ds(0, chips - 1)], par_sem.at[0])
    for half in range(2):
        wait_bytes(st_out.at[half, pl.ds(0, chips - 1)], st_sem.at[half, 0])
        wait_bytes(ready.at[half, pl.ds(0, chips - 1)], back_sem.at[half, 0])
        wait_bytes(grad_out.at[half, pl.ds(0, chips - 1)], grad_sem.at[half, 0])
    for n in range(3):
        wait_bytes(stage.at[0], out_sem.at[n])
    swap.wait()
    total_ref[...] = mine[...] + theirs[...]


def body(query, key_in, value_in, cotangent, residue, log_rate, bias):
    shards = lax.axis_size("ctx")
    channels, width = query.shape
    rate = jnp.exp(log_rate)
    root = jnp.sqrt(-jnp.expm1(-2.0 * rate))
    bias_rows = jnp.stack([bias, jnp.roll(bias, W // 2)])
    bias_rows = jnp.pad(bias_rows, ((0, 6), (0, LANES - W)))
    own = jnp.concatenate(
        [
            rate.reshape(HALF, LANES),
            (residue * root).reshape(HALF, LANES),
            bias_rows,
        ],
        axis=0,
    )
    vmem = pl.BlockSpec(memory_space=pltpu.VMEM)
    dma = pltpu.SemaphoreType.DMA

    def remote(number):
        return pltpu.CompilerParams(
            collective_id=number, has_side_effects=True, vmem_limit_bytes=52 * 1024 * 1024
        )

    chips = shards // 2
    split = lambda z: z.reshape(chips // 2, 2, 2, 2, W // 2, width)
    anywhere = pl.BlockSpec(memory_space=pl.ANY)
    part = jax.ShapeDtypeStruct((chips // 2, 2, 2, 2, W // 2, width), bf16)
    mixed, pgrad, total = pl.pallas_call(
        mixer_kernel,
        in_specs=[anywhere] * 5 + [vmem],
        out_specs=[anywhere, anywhere, vmem],
        out_shape=[part, part, jax.ShapeDtypeStruct((2, 16, LANES), f32)],
        scratch_shapes=[
            pltpu.VMEM((5 * W, LANES), f32),
            pltpu.VMEM((5 * W, LANES), bf16),
            pltpu.VMEM((2, 4, chips, 2, W // 2, W), bf16),
            pltpu.VMEM((2, chips, W, W), bf16),
            pltpu.VMEM((2, 2, chips, W, W), bf16),
            pltpu.VMEM((2, chips, W, W), bf16),
            pltpu.VMEM((2, chips, W, W), bf16),
            pltpu.VMEM((chips, 2 * HALF, W), f32),
            pltpu.VMEM((chips, 2, 16, LANES), bf16),
            pltpu.VMEM((chips, 10, HALF, LANES), f32),
            pltpu.VMEM((2, chips, HALF, LANES), f32),
            pltpu.VMEM((2, chips, HALF, LANES), f32),
            pltpu.VMEM((chips, HALF, LANES), f32),
            pltpu.VMEM((2, chips, HALF, LANES), f32),
            pltpu.VMEM((2, chips, HALF, LANES), f32),
            pltpu.VMEM((2, chips, 16, LANES), bf16),
            pltpu.VMEM((2, chips, 16, LANES), bf16),
            pltpu.VMEM((2, 16, LANES), f32),
            pltpu.VMEM((2, 16, LANES), f32),
            pltpu.VMEM((2, 2, chips, 2, W // 2, W), bf16),
            dma((3,)),
            dma((2,)),
            dma((5,)),
            dma((2, 2)),
            dma((2, 2)),
            dma((2, 2)),
            dma((3,)),
            dma((2,)),
        ],
        compiler_params=remote(1),
        name="mixer",
    )(split(query), split(key_in), split(value_in), split(cotangent), tables(), own)
    mixed = mixed.reshape(channels, width)
    pgrad = pgrad.reshape(channels, width)
    gated, gq = mul16(query, mixed), mul16(cotangent, mixed)
    gk, gv = mul16(pgrad, value_in), mul16(pgrad, key_in)

    modes = residue.shape[1]
    quad = HALF // 2
    grad_a = total[:, :quad].reshape(-1, modes)
    grad_d = total[:, quad : 2 * quad].reshape(-1, modes)
    skip = jnp.concatenate([total[0, HALF, : W // 2], total[1, HALF, W // 2 : W]])
    scale = 1.0 / math.sqrt(float(shards * width * lax.axis_size("dp")))
    grad_residue = root * grad_a * scale
    grad_rate = rate * residue * (jnp.exp(-2.0 * rate) / root * grad_a - root * grad_d) * scale
    grad_bias = skip * scale
    return gated, gq, gk, gv, grad_residue, grad_rate, grad_bias


def solution(mesh):
    tok = P(None, ("dp", "ctx"))
    chan = P("ctx", None)
    return jax.shard_map(
        body,
        mesh=mesh,
        in_specs=(tok, tok, tok, tok, chan, chan, P("ctx")),
        out_specs=(tok, tok, tok, tok, chan, chan, P("ctx")),
        check_vma=False,
    )
```

```python
import functools
import math

import jax
import jax.numpy as jnp
import numpy as np
from jax import lax
from jax.experimental import pallas as pl
from jax.experimental.pallas import tpu as pltpu
from jax.sharding import PartitionSpec as P

bf16 = jnp.bfloat16
f32 = jnp.float32
W = 128
HALF = 8
MESH = pl.DeviceIdType.MESH
LANES = 256


def table():
    n = np.arange(W)[:, None]
    f = np.arange(W)[None, :]
    angle = ((2 * f + 1) * n % (4 * W)) * (2.0 * math.pi / (4 * W))
    return jnp.asarray(np.concatenate([np.cos(angle), -np.sin(angle)], axis=1), f32)


def dot(a, b):
    return jnp.dot(a, b, preferred_element_type=f32)


def dot_nt(a, b):
    return lax.dot_general(a, b, (((1,), (1,)), ((), ())), preferred_element_type=f32)


def powers(rate_row):
    rate8 = jnp.broadcast_to(rate_row, (8, LANES))
    row = lax.broadcasted_iota(jnp.int32, (8, LANES), 0).astype(f32)
    out = jnp.exp(-rate8 * row)
    for step in (8, 16, 32, 64):
        mult = jnp.exp(-rate8 * float(step))
        parts = [out[i : i + 8] * mult for i in range(0, step, 8)]
        out = jnp.concatenate([out] + parts, axis=0)
    return out.astype(bf16)


def diag_mask():
    row = lax.broadcasted_iota(jnp.int32, (16, LANES), 0)
    lane = lax.broadcasted_iota(jnp.int32, (16, LANES), 1)
    return row == lane // 16


def diag_row(mask, rows):
    return jnp.sum(jnp.where(mask, rows, 0.0), axis=0, keepdims=True)


def mul16(a, b):
    return (a.astype(f32) * b.astype(f32)).astype(bf16)


def cmul(a, b):
    ar, ai, br, bi = a[:, :W], a[:, W:], b[:, :W], b[:, W:]
    return jnp.concatenate([ar * br - ai * bi, ar * bi + ai * br], axis=1).astype(bf16)


def wait_bytes(ref, sem):
    pltpu.make_async_copy(ref, ref, sem).wait()


def mixer_kernel(
    q_hbm, k_hbm, v_hbm, c_hbm, tab_ref, rate_ref, weight_ref, bias_ref,
    mixed_ref, pgrad_ref, total_ref,
    fwd_ref, fwdr_ref, inv_ref, invr_ref, flip_ref, inp, away, sig, rev, lags, skip, par, keep, st_out, came, hold, ready, got,
    grad_out, grad_in, mine, theirs, stage,
    load_sem, par_sem, pair_sem, st_sem, back_sem, grad_sem, out_sem, twin_sem,
):
    pairs = q_hbm.shape[0]
    chips = 2 * pairs
    steps = pairs // 2
    quad = HALF // 2
    me = lax.axis_index("ctx")
    core, chip = lax.rem(me, 2), lax.div(me, 2)
    near = {"ctx": me + 1 - 2 * core}
    twin = {"dp": 1 - lax.axis_index("dp")}

    def peer(b):
        return {"ctx": 2 * b + core}

    def after(i):
        return lax.rem(chip + i, chips)

    def remote(src, dst, send, recv, who):
        return pltpu.make_async_remote_copy(
            src_ref=src, dst_ref=dst, send_sem=send, recv_sem=recv,
            device_id=who, device_id_type=MESH,
        )

    for order in range(2):
        side = 1 - core if order == 0 else core
        for half in range(2):
            for n, ref in enumerate((q_hbm, k_hbm, v_hbm, c_hbm)):
                pltpu.make_async_copy(
                    ref.at[:, :, side, half], inp.at[order, n, pl.ds(half * pairs, pairs)],
                    load_sem.at[order],
                ).start()

    barrier = pltpu.get_barrier_semaphore()

    def tell(i, carry):
        pl.semaphore_signal(barrier, inc=1, device_id=peer(after(i)), device_id_type=MESH)
        return carry

    lax.fori_loop(1, chips, tell, 0)
    pl.semaphore_signal(barrier, inc=1, device_id=near, device_id_type=MESH)
    pl.semaphore_signal(barrier, inc=1, device_id=twin, device_id_type=MESH)

    own_rate, own_weight = rate_ref[...], weight_ref[...]
    own_bias = jnp.broadcast_to(bias_ref[...], (HALF, W))
    own_bias = jnp.concatenate([own_bias, pltpu.roll(own_bias, W // 2, 1)], axis=1)
    own_bias = [own_bias[:1], pltpu.roll(own_bias, W, 1)[:1]]
    lower = lambda z: z - z.astype(bf16).astype(f32)
    for half in range(2):
        rows = slice(quad * half, quad * half + quad)
        par[chip, half] = jnp.concatenate(
            [
                own_rate[rows],
                lower(own_rate)[rows],
                own_weight[rows],
                own_bias[half],
                lower(own_bias[half]),
                own_bias[1 - half],
                lower(own_bias[1 - half]),
            ],
            axis=0,
        ).astype(bf16)

    row_no = lax.broadcasted_iota(jnp.int32, (W, W), 0)
    lane_no = lax.broadcasted_iota(jnp.int32, (W, W), 1)
    fwd = tab_ref[...]
    flip = (row_no + lane_no == W - 1).astype(f32).astype(bf16)
    inv = (jnp.transpose(fwd) * (1.0 / W)).astype(bf16)
    fwd = fwd.astype(bf16)
    flip_ref[...] = flip
    fwd_ref[...] = fwd
    inv_ref[...] = inv
    fwdr_ref[...] = dot(flip, fwd).astype(bf16)
    invr_ref[...] = dot(inv, flip).astype(bf16)

    pieces = 4
    count = chips // pieces

    def products(order, dst, first):
        def step(i, carry):
            for v in [first + 4 * i + n for n in range(4)]:
                dst[0, v] = mul16(inp[order, 1, v], inp[order, 2, v]).reshape(W, W)
                dst[1, v] = mul16(inp[order, 3, v], inp[order, 0, v]).reshape(W, W)
            return carry

        lax.fori_loop(0, count // 4, step, 0)

    def send_par(i, carry):
        remote(
            par.at[chip], par.at[chip], par_sem.at[0], par_sem.at[1], peer(after(i))
        ).start()
        return carry

    wait_bytes(inp.at[0], load_sem.at[0])
    for n in range(pieces):
        products(0, away, n * count)
        if n == 0:
            pl.semaphore_wait(barrier, chips + 1)
            lax.fori_loop(1, chips, send_par, 0)
        block = pl.ds(n * count, count)
        remote(
            away.at[:, block], sig.at[core, :, block], pair_sem.at[pieces], pair_sem.at[n], near
        ).start()
    wait_bytes(inp.at[1], load_sem.at[1])
    for n in range(pieces):
        products(1, sig.at[core], n * count)

    eye = row_no == lane_no
    swapped_eye = lax.rem(row_no + W // 2, W) == lane_no
    lane = lax.broadcasted_iota(jnp.int32, (W, W), 1).astype(f32)
    mask = diag_mask()

    def local_lags(first, some):
        blocks = [first + n for n in range(some)]
        xs = [jnp.concatenate([sig[0, 0, v], sig[1, 0, v]], axis=0) for v in blocks]
        ms = [jnp.concatenate([sig[0, 1, v], sig[1, 1, v]], axis=0) for v in blocks]
        spec_x = [dot(x, fwd_ref[...]) for x in xs]
        spec_m = [dot(m, fwdr_ref[...]) for m in ms]
        turned = [dot(x, flip_ref[...]).astype(bf16) for x in xs]
        found = [dot(cmul(a, b), invr_ref[...]) for a, b in zip(spec_x, spec_m)]
        for n, v in enumerate(blocks):
            rev[0, v] = turned[n][:W]
            rev[1, v] = turned[n][W:]
            lag = found[n][:W] + found[n][W:]
            lags[0, v] = lag.astype(bf16)
            lags[1, v] = (lag * lane).astype(bf16)
            xm = xs[n].astype(f32) * ms[n].astype(f32)
            sums = jnp.sum(xm[:W] + xm[W:], axis=1, keepdims=True)
            for side, where in enumerate((eye, swapped_eye)):
                skip[v, HALF * side : HALF * side + HALF] = jnp.broadcast_to(
                    jnp.sum(jnp.where(where, sums, 0.0), axis=0, keepdims=True), (HALF, W)
                )

    def lags_of(half):
        for n in range(half * pieces // 2, (half + 1) * pieces // 2):
            block = pl.ds(n * count, count)
            wait_bytes(sig.at[core, :, block], pair_sem.at[n])

            def step(i, carry, n=n):
                local_lags(n * count + 4 * i, 4)
                return carry

            lax.fori_loop(0, count // 4, step, 0)

    lags_of(0)
    wait_bytes(par.at[pl.ds(0, chips - 1)], par_sem.at[1])

    def place(j, n):
        half = lax.div(j, steps)
        u = lax.rem(lax.div(chip, 2) + 2 * lax.rem(j, steps) + 1 + n, pairs)
        return half, u, half * pairs + u

    def halves(first, second, start):
        rows = slice(start, start + quad)
        return jnp.concatenate([first[rows], second[rows]], axis=0)

    def get_par(half, u):
        return par[2 * u, half].astype(f32), par[2 * u + 1, half].astype(f32)

    def get_rate(pair):
        return halves(*pair, 0) + halves(*pair, quad)

    def mode_sums(half, u, v):
        rate = get_rate(get_par(half, u))
        far = jnp.exp(-float(W) * rate)
        parts = [rev[0, v], rev[1, v], sig[0, 1, v], sig[1, 1, v], lags[0, v], lags[1, v]]
        for chunk in range(2):
            parts.append((parts[2 + chunk].astype(f32) * (lane + 1.0)).astype(bf16))
            parts.append((parts[chunk].astype(f32) * lane).astype(bf16))
        found = [[] for _ in parts]
        for g in range(HALF):
            e = powers(rate[g : g + 1])
            rows = slice(16 * g, 16 * g + 16)
            res = dot(jnp.concatenate([part[rows] for part in parts], axis=0), e)
            for n in range(len(parts)):
                found[n].append(diag_row(mask, res[16 * n : 16 * n + 16]))
        found = [jnp.concatenate(rows, axis=0) for rows in found]
        return found, found[0] * far + found[1], found[2] + far * found[3]

    def sum_step(j, carry):
        places = [place(j, n) for n in range(2)]
        results = [mode_sums(*where) for where in places]
        for (half, u, v), (found, ahead, back) in zip(places, results):
            for n, value in enumerate(found):
                keep[v, n] = value
            for n in range(2):
                rows = slice(quad * n, quad * n + quad)
                st_out[half, 2 * u + n] = jnp.concatenate([ahead[rows], back[rows]], axis=0)
        for half, u, v in places:
            for n in range(2):
                b = 2 * u + n

                @pl.when(b != chip)
                def _(b=b, half=half):
                    remote(
                        st_out.at[half, b], came.at[half, chip], st_sem.at[half, 0],
                        st_sem.at[half, 1], peer(b),
                    ).start()

        return carry

    def scan(half):
        came[half, chip] = st_out[half, chip]
        wait_bytes(came.at[half, pl.ds(0, chips - 1)], st_sem.at[half, 1])
        decay2 = jnp.exp(-2.0 * float(W) * own_rate[quad * half : quad * half + quad])

        def ahead(p, s):
            hold[p, 0:quad] = s
            return s * decay2 + came[half, p][:quad]

        lax.fori_loop(0, chips, ahead, jnp.zeros((quad, LANES), f32), unroll=8)

        def back(i, s):
            p = chips - 1 - i
            ready[half, p] = jnp.concatenate([hold[p, 0:quad], s], axis=0)
            return s * decay2 + came[half, p][quad:]

        lax.fori_loop(0, chips, back, jnp.zeros((quad, LANES), f32), unroll=8)

        def send_back(i, carry):
            b = after(i)
            remote(
                ready.at[half, b], got.at[half, chip], back_sem.at[half, 0], back_sem.at[half, 1],
                peer(b),
            ).start()
            return carry

        lax.fori_loop(1, chips, send_back, 0)
        got[half, chip] = ready[half, chip]

    def chunk_states(half, u, v, rate):
        pair = got[half, 2 * u], got[half, 2 * u + 1]
        far = jnp.exp(-float(W) * rate)
        s0, r1 = halves(*pair, 0), halves(*pair, quad)
        return s0, far * s0 + keep[v, 0], far * r1 + keep[v, 3], r1

    def send_grads(half):
        wait_bytes(got.at[half, pl.ds(0, chips - 1)], back_sem.at[half, 1])

        def made(u, v):
            rate = get_rate(get_par(half, u))
            near_decay = jnp.exp(-rate)
            s0, s1, r0, r1 = chunk_states(half, u, v, rate)
            grad_a = keep[v, 4] + near_decay * (keep[v, 2] * s0 + keep[v, 3] * s1)
            grad_d = keep[v, 5] + near_decay * (
                float(W) * jnp.exp(-float(W) * rate) * (s0 * r0 + s1 * r1)
                + s0 * keep[v, 6] + r0 * keep[v, 7] + s1 * keep[v, 8] + r1 * keep[v, 9]
            )
            messages = []
            for n in range(2):
                rows = slice(quad * n, quad * n + quad)
                first = 0 if n == half else HALF
                skip_part = jnp.concatenate(
                    [skip[v, first : first + HALF], jnp.zeros((HALF, W), f32)], axis=1
                )
                messages.append(
                    jnp.concatenate([grad_a[rows], grad_d[rows], skip_part], axis=0).astype(bf16)
                )
            return messages

        def step(i, carry):
            us = [lax.rem(lax.div(chip, 2) + 1 + 4 * i + n, pairs) for n in range(4)]
            results = [made(u, half * pairs + u) for u in us]
            for u, messages in zip(us, results):
                for n in range(2):
                    grad_out[half, 2 * u + n] = messages[n]
            for u in us:
                for n in range(2):
                    b = 2 * u + n

                    @pl.when(b != chip)
                    def _(b=b):
                        remote(
                            grad_out.at[half, b], grad_in.at[half, chip], grad_sem.at[half, 0],
                            grad_sem.at[half, 1], peer(b),
                        ).start()

            return carry

        lax.fori_loop(0, pairs // 4, step, 0)
        grad_in[half, chip] = grad_out[half, chip]

    def expand(half, u, v):
        pair = get_par(half, u)
        rate, weight = get_rate(pair), halves(*pair, 2 * quad)
        s0, s1, r0, r1 = chunk_states(half, u, v, rate)
        wa = weight * jnp.exp(-rate)
        terms = [weight, wa * s0, wa * s1, wa * r0, wa * r1]
        made = []
        for g in range(HALF):
            e = powers(rate[g : g + 1])
            lhs = jnp.concatenate(
                [jnp.where(mask, term[g : g + 1], 0.0) for term in terms], axis=0
            ).astype(bf16)
            made.append(dot_nt(lhs, e))
        return [jnp.concatenate([z[16 * n : 16 * n + 16] for z in made], axis=0) for n in range(5)]

    def convolve(half, u, v, taps, y0, y1, p0, p1):
        pair = get_par(half, u)
        even, odd = pair[0][12:13, :W] + pair[0][13:14, :W], pair[1][14:15, :W] + pair[1][15:, :W]
        bias_row = jnp.where(lane[:1] < W // 2, even, odd)
        x = jnp.concatenate([sig[0, 0, v], sig[1, 0, v]], axis=0)
        m = jnp.concatenate([sig[0, 1, v], sig[1, 1, v]], axis=0)
        spec_x, spec_m = dot(x, fwd_ref[...]), dot(m, fwdr_ref[...])
        spec_h = dot(taps.astype(bf16), fwd_ref[...])
        spec_h = jnp.concatenate([spec_h, spec_h], axis=0)
        gain = jnp.sum(jnp.where(eye, bias_row, 0.0), axis=1, keepdims=True)
        gain = jnp.concatenate([gain, gain], axis=0)
        y = dot(cmul(spec_x, spec_h), inv_ref[...])
        y += jnp.concatenate([y0, y1], axis=0) + gain * x.astype(f32)
        p = dot(cmul(spec_m, spec_h), invr_ref[...])
        p += dot(jnp.concatenate([p0, p1], axis=0).astype(bf16), flip_ref[...])
        p += gain * m.astype(f32)
        return y.astype(bf16), p.astype(bf16)

    def finish(j, carry):
        places = [place(j, n) for n in range(2)]
        grown = [expand(*where) for where in places]
        results = [convolve(*where, *terms) for where, terms in zip(places, grown)]
        for (half, u, v), result in zip(places, results):
            for n, out in enumerate((mixed_ref, pgrad_ref)):
                both = [
                    result[n][W * chunk : W * chunk + W].reshape(2, W // 2, W) for chunk in range(2)
                ]
                mine_first = core == 0
                kept = jnp.where(mine_first, both[0], both[1])
                stage[n, v] = jnp.where(mine_first, both[1], both[0])
                for side in range(2):
                    out[u, side, core, half] = kept[side]
        for half, u, v in places:
            for n, out in enumerate((mixed_ref, pgrad_ref)):
                remote(
                    stage.at[n, v], out.at[u, :, core, half], out_sem.at[0], out_sem.at[1], near
                ).start()
        return carry

    middle = steps + steps // 8
    lax.fori_loop(0, steps, sum_step, 0)
    lags_of(1)
    lax.fori_loop(steps, middle, sum_step, 0)
    scan(0)
    lax.fori_loop(middle, 2 * steps, sum_step, 0)
    send_grads(0)
    lax.fori_loop(0, steps // 4, finish, 0)
    scan(1)
    lax.fori_loop(steps // 4, steps, finish, 0)
    send_grads(1)
    early = steps + 3 * steps // 4
    lax.fori_loop(steps, early, finish, 0)
    for half in range(2):
        wait_bytes(grad_in.at[half, pl.ds(0, chips - 1)], grad_sem.at[half, 1])
        mine[half] = lax.fori_loop(
            0, chips, lambda p, t: t + grad_in[half, p].astype(f32), jnp.zeros((16, LANES), f32),
            unroll=8,
        )
    swap = remote(mine, theirs, twin_sem.at[0], twin_sem.at[1], twin)
    swap.start()
    lax.fori_loop(early, 2 * steps, finish, 0)
    wait_bytes(away, pair_sem.at[pieces])
    wait_bytes(par.at[pl.ds(0, chips - 1)], par_sem.at[0])
    for half in range(2):
        wait_bytes(st_out.at[half, pl.ds(0, chips - 1)], st_sem.at[half, 0])
        wait_bytes(ready.at[half, pl.ds(0, chips - 1)], back_sem.at[half, 0])
        wait_bytes(grad_out.at[half, pl.ds(0, chips - 1)], grad_sem.at[half, 0])
    for n in range(2):
        wait_bytes(stage, out_sem.at[n])
    swap.wait()
    total_ref[...] = mine[...] + theirs[...]


def body(query, key_in, value_in, cotangent, residue, log_rate, bias):
    shards = lax.axis_size("ctx")
    channels, width = query.shape
    rate = jnp.exp(log_rate)
    root = jnp.sqrt(-jnp.expm1(-2.0 * rate))
    rate_rows = rate.reshape(HALF, LANES)
    weight_rows = (residue * root).reshape(HALF, LANES)
    vmem = pl.BlockSpec(memory_space=pltpu.VMEM)
    dma = pltpu.SemaphoreType.DMA

    def remote(number):
        return pltpu.CompilerParams(
            collective_id=number, has_side_effects=True, vmem_limit_bytes=52 * 1024 * 1024
        )

    chips = shards // 2
    split = lambda z: z.reshape(chips // 2, 2, 2, 2, W // 2, width)
    anywhere = pl.BlockSpec(memory_space=pl.ANY)
    part = jax.ShapeDtypeStruct((chips // 2, 2, 2, 2, W // 2, width), bf16)
    mixed, pgrad, total = pl.pallas_call(
        mixer_kernel,
        in_specs=[anywhere] * 4 + [vmem] * 4,
        out_specs=[vmem] * 3,
        out_shape=[part, part, jax.ShapeDtypeStruct((2, 16, LANES), f32)],
        scratch_shapes=[
            pltpu.VMEM((W, 2 * W), bf16),
            pltpu.VMEM((W, 2 * W), bf16),
            pltpu.VMEM((2 * W, W), bf16),
            pltpu.VMEM((2 * W, W), bf16),
            pltpu.VMEM((W, W), bf16),
            pltpu.VMEM((2, 4, chips, 2, W // 2, W), bf16),
            pltpu.VMEM((2, chips, W, W), bf16),
            pltpu.VMEM((2, 2, chips, W, W), bf16),
            pltpu.VMEM((2, chips, W, W), bf16),
            pltpu.VMEM((2, chips, W, W), bf16),
            pltpu.VMEM((chips, 2 * HALF, W), f32),
            pltpu.VMEM((chips, 2, 16, LANES), bf16),
            pltpu.VMEM((chips, 10, HALF, LANES), f32),
            pltpu.VMEM((2, chips, HALF, LANES), f32),
            pltpu.VMEM((2, chips, HALF, LANES), f32),
            pltpu.VMEM((chips, HALF, LANES), f32),
            pltpu.VMEM((2, chips, HALF, LANES), f32),
            pltpu.VMEM((2, chips, HALF, LANES), f32),
            pltpu.VMEM((2, chips, 16, LANES), bf16),
            pltpu.VMEM((2, chips, 16, LANES), bf16),
            pltpu.VMEM((2, 16, LANES), f32),
            pltpu.VMEM((2, 16, LANES), f32),
            pltpu.VMEM((2, chips, 2, W // 2, W), bf16),
            dma((2,)),
            dma((2,)),
            dma((5,)),
            dma((2, 2)),
            dma((2, 2)),
            dma((2, 2)),
            dma((2,)),
            dma((2,)),
        ],
        compiler_params=remote(1),
        name="mixer",
    )(split(query), split(key_in), split(value_in), split(cotangent), table(), rate_rows,
      weight_rows, bias.reshape(1, W))
    mixed = mixed.reshape(channels, width)
    pgrad = pgrad.reshape(channels, width)
    gated, gq = mul16(query, mixed), mul16(cotangent, mixed)
    gk, gv = mul16(pgrad, value_in), mul16(pgrad, key_in)

    modes = residue.shape[1]
    quad = HALF // 2
    grad_a = total[:, :quad].reshape(-1, modes)
    grad_d = total[:, quad : 2 * quad].reshape(-1, modes)
    skip = jnp.concatenate([total[0, HALF, : W // 2], total[1, HALF, W // 2 : W]])
    scale = 1.0 / math.sqrt(float(shards * width * lax.axis_size("dp")))
    grad_residue = root * grad_a * scale
    grad_rate = rate * residue * (jnp.exp(-2.0 * rate) / root * grad_a - root * grad_d) * scale
    grad_bias = skip * scale
    return gated, gq, gk, gv, grad_residue, grad_rate, grad_bias


def solution(mesh):
    tok = P(None, ("dp", "ctx"))
    chan = P("ctx", None)
    return jax.shard_map(
        body,
        mesh=mesh,
        in_specs=(tok, tok, tok, tok, chan, chan, P("ctx")),
        out_specs=(tok, tok, tok, tok, chan, chan, P("ctx")),
        check_vma=False,
    )
```

```python
import functools
import math

import jax
import jax.numpy as jnp
import numpy as np
from jax import lax
from jax.experimental import pallas as pl
from jax.experimental.pallas import tpu as pltpu
from jax.sharding import PartitionSpec as P

bf16 = jnp.bfloat16
f32 = jnp.float32
W = 128
HALF = 8
MESH = pl.DeviceIdType.MESH
LANES = 256


def table():
    n = np.arange(W)[:, None]
    f = np.arange(W)[None, :]
    angle = ((2 * f + 1) * n % (4 * W)) * (2.0 * math.pi / (4 * W))
    return jnp.asarray(np.concatenate([np.cos(angle), -np.sin(angle)], axis=1), f32)


def dot(a, b):
    return jnp.dot(a, b, preferred_element_type=f32)


def dot_nt(a, b):
    return lax.dot_general(a, b, (((1,), (1,)), ((), ())), preferred_element_type=f32)


def powers(rate_row):
    rate8 = jnp.broadcast_to(rate_row, (8, LANES))
    row = lax.broadcasted_iota(jnp.int32, (8, LANES), 0).astype(f32)
    out = jnp.exp(-rate8 * row)
    for step in (8, 16, 32, 64):
        mult = jnp.exp(-rate8 * float(step))
        parts = [out[i : i + 8] * mult for i in range(0, step, 8)]
        out = jnp.concatenate([out] + parts, axis=0)
    return out.astype(bf16)


def diag_mask():
    row = lax.broadcasted_iota(jnp.int32, (16, LANES), 0)
    lane = lax.broadcasted_iota(jnp.int32, (16, LANES), 1)
    return row == lane // 16


def diag_row(mask, rows):
    return jnp.sum(jnp.where(mask, rows, 0.0), axis=0, keepdims=True)


def mul16(a, b):
    return (a.astype(f32) * b.astype(f32)).astype(bf16)


def cmul(a, b):
    ar, ai, br, bi = a[:, :W], a[:, W:], b[:, :W], b[:, W:]
    return jnp.concatenate([ar * br - ai * bi, ar * bi + ai * br], axis=1).astype(bf16)


def wait_bytes(ref, sem):
    pltpu.make_async_copy(ref, ref, sem).wait()


def mixer_kernel(
    q_hbm, k_hbm, v_hbm, c_hbm, tab_ref, rate_ref, weight_ref, bias_ref,
    mixed_ref, pgrad_ref, total_ref,
    fwd_ref, fwdr_ref, inv_ref, invr_ref, flip_ref, inp, away, sig, rev, lags, skip, par, keep, st_out, came, hold, ready, got,
    grad_out, grad_in, mine, theirs, stage,
    load_sem, par_sem, pair_sem, st_sem, back_sem, grad_sem, out_sem, twin_sem,
):
    pairs = q_hbm.shape[0]
    chips = 2 * pairs
    steps = pairs // 2
    quad = HALF // 2
    me = lax.axis_index("ctx")
    core, chip = lax.rem(me, 2), lax.div(me, 2)
    near = {"ctx": me + 1 - 2 * core}
    twin = {"dp": 1 - lax.axis_index("dp")}

    def peer(b):
        return {"ctx": 2 * b + core}

    def after(i):
        return lax.rem(chip + i, chips)

    def remote(src, dst, send, recv, who):
        return pltpu.make_async_remote_copy(
            src_ref=src, dst_ref=dst, send_sem=send, recv_sem=recv,
            device_id=who, device_id_type=MESH,
        )

    for order in range(2):
        side = 1 - core if order == 0 else core
        for half in range(2):
            for n, ref in enumerate((q_hbm, k_hbm, v_hbm, c_hbm)):
                pltpu.make_async_copy(
                    ref.at[:, :, side, half], inp.at[order, n, pl.ds(half * pairs, pairs)],
                    load_sem.at[order],
                ).start()

    barrier = pltpu.get_barrier_semaphore()

    def tell(i, carry):
        pl.semaphore_signal(barrier, inc=1, device_id=peer(after(i)), device_id_type=MESH)
        return carry

    lax.fori_loop(1, chips, tell, 0)
    pl.semaphore_signal(barrier, inc=1, device_id=near, device_id_type=MESH)
    pl.semaphore_signal(barrier, inc=1, device_id=twin, device_id_type=MESH)

    own_rate, own_weight = rate_ref[...], weight_ref[...]
    own_bias = jnp.broadcast_to(bias_ref[...], (HALF, W))
    own_bias = jnp.concatenate([own_bias, pltpu.roll(own_bias, W // 2, 1)], axis=1)
    own_bias = [own_bias[:1], pltpu.roll(own_bias, W, 1)[:1]]
    lower = lambda z: z - z.astype(bf16).astype(f32)
    for half in range(2):
        rows = slice(quad * half, quad * half + quad)
        par[chip, half] = jnp.concatenate(
            [
                own_rate[rows],
                lower(own_rate)[rows],
                own_weight[rows],
                own_bias[half],
                lower(own_bias[half]),
                own_bias[1 - half],
                lower(own_bias[1 - half]),
            ],
            axis=0,
        ).astype(bf16)

    row_no = lax.broadcasted_iota(jnp.int32, (W, W), 0)
    lane_no = lax.broadcasted_iota(jnp.int32, (W, W), 1)
    fwd = tab_ref[...]
    flip = (row_no + lane_no == W - 1).astype(f32).astype(bf16)
    inv = (jnp.transpose(fwd) * (1.0 / W)).astype(bf16)
    fwd = fwd.astype(bf16)
    flip_ref[...] = flip
    fwd_ref[...] = fwd
    inv_ref[...] = inv
    fwdr_ref[...] = dot(flip, fwd).astype(bf16)
    invr_ref[...] = dot(inv, flip).astype(bf16)

    pieces = 4
    count = chips // pieces

    def products(order, dst, first):
        def step(i, carry):
            for v in [first + 4 * i + n for n in range(4)]:
                dst[0, v] = mul16(inp[order, 1, v], inp[order, 2, v]).reshape(W, W)
                dst[1, v] = mul16(inp[order, 3, v], inp[order, 0, v]).reshape(W, W)
            return carry

        lax.fori_loop(0, count // 4, step, 0)

    def send_par(i, carry):
        remote(
            par.at[chip], par.at[chip], par_sem.at[0], par_sem.at[1], peer(after(i))
        ).start()
        return carry

    wait_bytes(inp.at[0], load_sem.at[0])
    for n in range(pieces):
        products(0, away, n * count)
        if n == 0:
            pl.semaphore_wait(barrier, chips + 1)
            lax.fori_loop(1, chips, send_par, 0)
        block = pl.ds(n * count, count)
        remote(
            away.at[:, block], sig.at[core, :, block], pair_sem.at[pieces], pair_sem.at[n], near
        ).start()
    wait_bytes(inp.at[1], load_sem.at[1])
    for n in range(pieces):
        products(1, sig.at[core], n * count)

    eye = row_no == lane_no
    swapped_eye = lax.rem(row_no + W // 2, W) == lane_no
    lane = lax.broadcasted_iota(jnp.int32, (W, W), 1).astype(f32)
    mask = diag_mask()

    def local_lags(first, some):
        blocks = [first + n for n in range(some)]
        xs = [jnp.concatenate([sig[0, 0, v], sig[1, 0, v]], axis=0) for v in blocks]
        ms = [jnp.concatenate([sig[0, 1, v], sig[1, 1, v]], axis=0) for v in blocks]
        spec_x = [dot(x, fwd_ref[...]) for x in xs]
        spec_m = [dot(m, fwdr_ref[...]) for m in ms]
        turned = [dot(x, flip_ref[...]).astype(bf16) for x in xs]
        found = [dot(cmul(a, b), invr_ref[...]) for a, b in zip(spec_x, spec_m)]
        for n, v in enumerate(blocks):
            rev[0, v] = turned[n][:W]
            rev[1, v] = turned[n][W:]
            lag = found[n][:W] + found[n][W:]
            lags[0, v] = lag.astype(bf16)
            lags[1, v] = (lag * lane).astype(bf16)
            xm = xs[n].astype(f32) * ms[n].astype(f32)
            sums = jnp.sum(xm[:W] + xm[W:], axis=1, keepdims=True)
            for side, where in enumerate((eye, swapped_eye)):
                skip[v, HALF * side : HALF * side + HALF] = jnp.broadcast_to(
                    jnp.sum(jnp.where(where, sums, 0.0), axis=0, keepdims=True), (HALF, W)
                )

    def lags_of(half):
        for n in range(half * pieces // 2, (half + 1) * pieces // 2):
            block = pl.ds(n * count, count)
            wait_bytes(sig.at[core, :, block], pair_sem.at[n])

            def step(i, carry, n=n):
                local_lags(n * count + 4 * i, 4)
                return carry

            lax.fori_loop(0, count // 4, step, 0)

    lags_of(0)
    lags_of(1)
    wait_bytes(par.at[pl.ds(0, chips - 1)], par_sem.at[1])

    def place(j, n):
        half = lax.div(j, steps)
        u = lax.rem(lax.div(chip, 2) + 2 * lax.rem(j, steps) + 1 + n, pairs)
        return half, u, half * pairs + u

    def halves(first, second, start):
        rows = slice(start, start + quad)
        return jnp.concatenate([first[rows], second[rows]], axis=0)

    def get_par(half, u):
        return par[2 * u, half].astype(f32), par[2 * u + 1, half].astype(f32)

    def get_rate(pair):
        return halves(*pair, 0) + halves(*pair, quad)

    def mode_sums(half, u, v):
        rate = get_rate(get_par(half, u))
        far = jnp.exp(-float(W) * rate)
        parts = [rev[0, v], rev[1, v], sig[0, 1, v], sig[1, 1, v], lags[0, v], lags[1, v]]
        for chunk in range(2):
            parts.append((parts[2 + chunk].astype(f32) * (lane + 1.0)).astype(bf16))
            parts.append((parts[chunk].astype(f32) * lane).astype(bf16))
        found = [[] for _ in parts]
        for g in range(HALF):
            e = powers(rate[g : g + 1])
            rows = slice(16 * g, 16 * g + 16)
            res = dot(jnp.concatenate([part[rows] for part in parts], axis=0), e)
            for n in range(len(parts)):
                found[n].append(diag_row(mask, res[16 * n : 16 * n + 16]))
        found = [jnp.concatenate(rows, axis=0) for rows in found]
        return found, found[0] * far + found[1], found[2] + far * found[3]

    def sum_step(j, carry):
        places = [place(j, n) for n in range(2)]
        results = [mode_sums(*where) for where in places]
        for (half, u, v), (found, ahead, back) in zip(places, results):
            for n, value in enumerate(found):
                keep[v, n] = value
            for n in range(2):
                rows = slice(quad * n, quad * n + quad)
                st_out[half, 2 * u + n] = jnp.concatenate([ahead[rows], back[rows]], axis=0)
        for half, u, v in places:
            for n in range(2):
                b = 2 * u + n

                @pl.when(b != chip)
                def _(b=b, half=half):
                    remote(
                        st_out.at[half, b], came.at[half, chip], st_sem.at[half, 0],
                        st_sem.at[half, 1], peer(b),
                    ).start()

        return carry

    def scan(half):
        came[half, chip] = st_out[half, chip]
        wait_bytes(came.at[half, pl.ds(0, chips - 1)], st_sem.at[half, 1])
        decay2 = jnp.exp(-2.0 * float(W) * own_rate[quad * half : quad * half + quad])

        def ahead(p, s):
            hold[p, 0:quad] = s
            return s * decay2 + came[half, p][:quad]

        lax.fori_loop(0, chips, ahead, jnp.zeros((quad, LANES), f32), unroll=8)

        def back(i, s):
            p = chips - 1 - i
            ready[half, p] = jnp.concatenate([hold[p, 0:quad], s], axis=0)
            return s * decay2 + came[half, p][quad:]

        lax.fori_loop(0, chips, back, jnp.zeros((quad, LANES), f32), unroll=8)

        def send_back(i, carry):
            b = after(i)
            remote(
                ready.at[half, b], got.at[half, chip], back_sem.at[half, 0], back_sem.at[half, 1],
                peer(b),
            ).start()
            return carry

        lax.fori_loop(1, chips, send_back, 0)
        got[half, chip] = ready[half, chip]

    def chunk_states(half, u, v, rate):
        pair = got[half, 2 * u], got[half, 2 * u + 1]
        far = jnp.exp(-float(W) * rate)
        s0, r1 = halves(*pair, 0), halves(*pair, quad)
        return s0, far * s0 + keep[v, 0], far * r1 + keep[v, 3], r1

    def send_grads(half):
        wait_bytes(got.at[half, pl.ds(0, chips - 1)], back_sem.at[half, 1])

        def made(u, v):
            rate = get_rate(get_par(half, u))
            near_decay = jnp.exp(-rate)
            s0, s1, r0, r1 = chunk_states(half, u, v, rate)
            grad_a = keep[v, 4] + near_decay * (keep[v, 2] * s0 + keep[v, 3] * s1)
            grad_d = keep[v, 5] + near_decay * (
                float(W) * jnp.exp(-float(W) * rate) * (s0 * r0 + s1 * r1)
                + s0 * keep[v, 6] + r0 * keep[v, 7] + s1 * keep[v, 8] + r1 * keep[v, 9]
            )
            messages = []
            for n in range(2):
                rows = slice(quad * n, quad * n + quad)
                first = 0 if n == half else HALF
                skip_part = jnp.concatenate(
                    [skip[v, first : first + HALF], jnp.zeros((HALF, W), f32)], axis=1
                )
                messages.append(
                    jnp.concatenate([grad_a[rows], grad_d[rows], skip_part], axis=0).astype(bf16)
                )
            return messages

        def step(i, carry):
            us = [lax.rem(lax.div(chip, 2) + 1 + 4 * i + n, pairs) for n in range(4)]
            results = [made(u, half * pairs + u) for u in us]
            for u, messages in zip(us, results):
                for n in range(2):
                    grad_out[half, 2 * u + n] = messages[n]
            for u in us:
                for n in range(2):
                    b = 2 * u + n

                    @pl.when(b != chip)
                    def _(b=b):
                        remote(
                            grad_out.at[half, b], grad_in.at[half, chip], grad_sem.at[half, 0],
                            grad_sem.at[half, 1], peer(b),
                        ).start()

            return carry

        lax.fori_loop(0, pairs // 4, step, 0)
        grad_in[half, chip] = grad_out[half, chip]

    def expand(half, u, v):
        pair = get_par(half, u)
        rate, weight = get_rate(pair), halves(*pair, 2 * quad)
        s0, s1, r0, r1 = chunk_states(half, u, v, rate)
        wa = weight * jnp.exp(-rate)
        terms = [weight, wa * s0, wa * s1, wa * r0, wa * r1]
        made = []
        for g in range(HALF):
            e = powers(rate[g : g + 1])
            lhs = jnp.concatenate(
                [jnp.where(mask, term[g : g + 1], 0.0) for term in terms], axis=0
            ).astype(bf16)
            made.append(dot_nt(lhs, e))
        return [jnp.concatenate([z[16 * n : 16 * n + 16] for z in made], axis=0) for n in range(5)]

    def convolve(half, u, v, taps, y0, y1, p0, p1):
        pair = get_par(half, u)
        even, odd = pair[0][12:13, :W] + pair[0][13:14, :W], pair[1][14:15, :W] + pair[1][15:, :W]
        bias_row = jnp.where(lane[:1] < W // 2, even, odd)
        x = jnp.concatenate([sig[0, 0, v], sig[1, 0, v]], axis=0)
        m = jnp.concatenate([sig[0, 1, v], sig[1, 1, v]], axis=0)
        spec_x, spec_m = dot(x, fwd_ref[...]), dot(m, fwdr_ref[...])
        spec_h = dot(taps.astype(bf16), fwd_ref[...])
        spec_h = jnp.concatenate([spec_h, spec_h], axis=0)
        gain = jnp.sum(jnp.where(eye, bias_row, 0.0), axis=1, keepdims=True)
        gain = jnp.concatenate([gain, gain], axis=0)
        y = dot(cmul(spec_x, spec_h), inv_ref[...])
        y += jnp.concatenate([y0, y1], axis=0) + gain * x.astype(f32)
        p = dot(cmul(spec_m, spec_h), invr_ref[...])
        p += dot(jnp.concatenate([p0, p1], axis=0).astype(bf16), flip_ref[...])
        p += gain * m.astype(f32)
        return y.astype(bf16), p.astype(bf16)

    def finish(j, carry):
        places = [place(j, n) for n in range(2)]
        grown = [expand(*where) for where in places]
        results = [convolve(*where, *terms) for where, terms in zip(places, grown)]
        for (half, u, v), result in zip(places, results):
            for n, out in enumerate((mixed_ref, pgrad_ref)):
                both = [
                    result[n][W * chunk : W * chunk + W].reshape(2, W // 2, W) for chunk in range(2)
                ]
                mine_first = core == 0
                kept = jnp.where(mine_first, both[0], both[1])
                stage[n, v] = jnp.where(mine_first, both[1], both[0])
                for side in range(2):
                    out[u, side, core, half] = kept[side]
        for half, u, v in places:
            for n, out in enumerate((mixed_ref, pgrad_ref)):
                remote(
                    stage.at[n, v], out.at[u, :, core, half], out_sem.at[0], out_sem.at[1], near
                ).start()
        return carry

    middle = steps + 5 * steps // 8
    lax.fori_loop(0, steps, sum_step, 0)
    lax.fori_loop(steps, middle, sum_step, 0)
    scan(0)
    lax.fori_loop(middle, 2 * steps, sum_step, 0)
    send_grads(0)
    lax.fori_loop(0, steps // 4, finish, 0)
    scan(1)
    lax.fori_loop(steps // 4, steps, finish, 0)
    send_grads(1)
    early = steps + 3 * steps // 4
    lax.fori_loop(steps, early, finish, 0)
    for half in range(2):
        wait_bytes(grad_in.at[half, pl.ds(0, chips - 1)], grad_sem.at[half, 1])
        mine[half] = lax.fori_loop(
            0, chips, lambda p, t: t + grad_in[half, p].astype(f32), jnp.zeros((16, LANES), f32),
            unroll=8,
        )
    swap = remote(mine, theirs, twin_sem.at[0], twin_sem.at[1], twin)
    swap.start()
    lax.fori_loop(early, 2 * steps, finish, 0)
    wait_bytes(away, pair_sem.at[pieces])
    wait_bytes(par.at[pl.ds(0, chips - 1)], par_sem.at[0])
    for half in range(2):
        wait_bytes(st_out.at[half, pl.ds(0, chips - 1)], st_sem.at[half, 0])
        wait_bytes(ready.at[half, pl.ds(0, chips - 1)], back_sem.at[half, 0])
        wait_bytes(grad_out.at[half, pl.ds(0, chips - 1)], grad_sem.at[half, 0])
    for n in range(2):
        wait_bytes(stage, out_sem.at[n])
    swap.wait()
    total_ref[...] = mine[...] + theirs[...]


def body(query, key_in, value_in, cotangent, residue, log_rate, bias):
    shards = lax.axis_size("ctx")
    channels, width = query.shape
    rate = jnp.exp(log_rate)
    root = jnp.sqrt(-jnp.expm1(-2.0 * rate))
    rate_rows = rate.reshape(HALF, LANES)
    weight_rows = (residue * root).reshape(HALF, LANES)
    vmem = pl.BlockSpec(memory_space=pltpu.VMEM)
    dma = pltpu.SemaphoreType.DMA

    def remote(number):
        return pltpu.CompilerParams(
            collective_id=number, has_side_effects=True, vmem_limit_bytes=49 * 1024 * 1024
        )

    chips = shards // 2
    split = lambda z: z.reshape(chips // 2, 2, 2, 2, W // 2, width)
    anywhere = pl.BlockSpec(memory_space=pl.ANY)
    part = jax.ShapeDtypeStruct((chips // 2, 2, 2, 2, W // 2, width), bf16)
    mixed, pgrad, total = pl.pallas_call(
        mixer_kernel,
        in_specs=[anywhere] * 4 + [vmem] * 4,
        out_specs=[vmem] * 3,
        out_shape=[part, part, jax.ShapeDtypeStruct((2, 16, LANES), f32)],
        scratch_shapes=[
            pltpu.VMEM((W, 2 * W), bf16),
            pltpu.VMEM((W, 2 * W), bf16),
            pltpu.VMEM((2 * W, W), bf16),
            pltpu.VMEM((2 * W, W), bf16),
            pltpu.VMEM((W, W), bf16),
            pltpu.VMEM((2, 4, chips, 2, W // 2, W), bf16),
            pltpu.VMEM((2, chips, W, W), bf16),
            pltpu.VMEM((2, 2, chips, W, W), bf16),
            pltpu.VMEM((2, chips, W, W), bf16),
            pltpu.VMEM((2, chips, W, W), bf16),
            pltpu.VMEM((chips, 2 * HALF, W), f32),
            pltpu.VMEM((chips, 2, 16, LANES), bf16),
            pltpu.VMEM((chips, 10, HALF, LANES), f32),
            pltpu.VMEM((2, chips, HALF, LANES), f32),
            pltpu.VMEM((2, chips, HALF, LANES), f32),
            pltpu.VMEM((chips, HALF, LANES), f32),
            pltpu.VMEM((2, chips, HALF, LANES), f32),
            pltpu.VMEM((2, chips, HALF, LANES), f32),
            pltpu.VMEM((2, chips, 16, LANES), bf16),
            pltpu.VMEM((2, chips, 16, LANES), bf16),
            pltpu.VMEM((2, 16, LANES), f32),
            pltpu.VMEM((2, 16, LANES), f32),
            pltpu.VMEM((2, chips, 2, W // 2, W), bf16),
            dma((2,)),
            dma((2,)),
            dma((5,)),
            dma((2, 2)),
            dma((2, 2)),
            dma((2, 2)),
            dma((2,)),
            dma((2,)),
        ],
        compiler_params=remote(1),
        name="mixer",
    )(split(query), split(key_in), split(value_in), split(cotangent), table(), rate_rows,
      weight_rows, bias.reshape(1, W))
    mixed = mixed.reshape(channels, width)
    pgrad = pgrad.reshape(channels, width)
    gated, gq = mul16(query, mixed), mul16(cotangent, mixed)
    gk, gv = mul16(pgrad, value_in), mul16(pgrad, key_in)

    modes = residue.shape[1]
    quad = HALF // 2
    grad_a = total[:, :quad].reshape(-1, modes)
    grad_d = total[:, quad : 2 * quad].reshape(-1, modes)
    skip = jnp.concatenate([total[0, HALF, : W // 2], total[1, HALF, W // 2 : W]])
    scale = 1.0 / math.sqrt(float(shards * width * lax.axis_size("dp")))
    grad_residue = root * grad_a * scale
    grad_rate = rate * residue * (jnp.exp(-2.0 * rate) / root * grad_a - root * grad_d) * scale
    grad_bias = skip * scale
    return gated, gq, gk, gv, grad_residue, grad_rate, grad_bias


def solution(mesh):
    tok = P(None, ("dp", "ctx"))
    chan = P("ctx", None)
    return jax.shard_map(
        body,
        mesh=mesh,
        in_specs=(tok, tok, tok, tok, chan, chan, P("ctx")),
        out_specs=(tok, tok, tok, tok, chan, chan, P("ctx")),
        check_vma=False,
    )
```

```python
import functools
import math

import jax
import jax.numpy as jnp
import numpy as np
from jax import lax
from jax.experimental import pallas as pl
from jax.experimental.pallas import tpu as pltpu
from jax.sharding import PartitionSpec as P

bf16 = jnp.bfloat16
f32 = jnp.float32
W = 128
HALF = 8
MESH = pl.DeviceIdType.MESH
LANES = 256


def table():
    n = np.arange(W)[:, None]
    f = np.arange(W)[None, :]
    angle = ((2 * f + 1) * n % (4 * W)) * (2.0 * math.pi / (4 * W))
    return jnp.asarray(np.concatenate([np.cos(angle), -np.sin(angle)], axis=1), f32)


def dot(a, b):
    return jnp.dot(a, b, preferred_element_type=f32)


def dot_nt(a, b):
    return lax.dot_general(a, b, (((1,), (1,)), ((), ())), preferred_element_type=f32)


def powers(rate_row):
    rate8 = jnp.broadcast_to(rate_row, (8, LANES))
    row = lax.broadcasted_iota(jnp.int32, (8, LANES), 0).astype(f32)
    out = jnp.exp(-rate8 * row)
    for step in (8, 16, 32, 64):
        mult = jnp.exp(-rate8 * float(step))
        parts = [out[i : i + 8] * mult for i in range(0, step, 8)]
        out = jnp.concatenate([out] + parts, axis=0)
    return out.astype(bf16)


def diag_mask():
    row = lax.broadcasted_iota(jnp.int32, (16, LANES), 0)
    lane = lax.broadcasted_iota(jnp.int32, (16, LANES), 1)
    return row == lane // 16


def diag_row(mask, rows):
    return jnp.sum(jnp.where(mask, rows, 0.0), axis=0, keepdims=True)


def mul16(a, b):
    return (a.astype(f32) * b.astype(f32)).astype(bf16)


def cmul(a, b):
    ar, ai, br, bi = a[:, :W], a[:, W:], b[:, :W], b[:, W:]
    return jnp.concatenate([ar * br - ai * bi, ar * bi + ai * br], axis=1).astype(bf16)


def wait_bytes(ref, sem):
    pltpu.make_async_copy(ref, ref, sem).wait()


def mixer_kernel(
    q_hbm, k_hbm, v_hbm, c_hbm, tab_ref, rate_ref, weight_ref, bias_ref,
    mixed_ref, pgrad_ref, total_ref,
    fwd_ref, fwdr_ref, inv_ref, invr_ref, flip_ref, inp, away, sig, rev, lags, skip, par, keep, st_out, came, hold, ready, got,
    grad_out, grad_in, mine, theirs, stage,
    load_sem, par_sem, pair_sem, st_sem, back_sem, grad_sem, out_sem, twin_sem,
):
    pairs = q_hbm.shape[0]
    chips = 2 * pairs
    steps = pairs // 2
    quad = HALF // 2
    me = lax.axis_index("ctx")
    core, chip = lax.rem(me, 2), lax.div(me, 2)
    near = {"ctx": me + 1 - 2 * core}
    twin = {"dp": 1 - lax.axis_index("dp")}

    def peer(b):
        return {"ctx": 2 * b + core}

    def after(i):
        return lax.rem(chip + i, chips)

    def remote(src, dst, send, recv, who):
        return pltpu.make_async_remote_copy(
            src_ref=src, dst_ref=dst, send_sem=send, recv_sem=recv,
            device_id=who, device_id_type=MESH,
        )

    for order in range(2):
        side = 1 - core if order == 0 else core
        for half in range(2):
            for n, ref in enumerate((q_hbm, k_hbm, v_hbm, c_hbm)):
                pltpu.make_async_copy(
                    ref.at[:, :, side, half], inp.at[order, n, pl.ds(half * pairs, pairs)],
                    load_sem.at[order],
                ).start()

    barrier = pltpu.get_barrier_semaphore()

    def tell(i, carry):
        pl.semaphore_signal(barrier, inc=1, device_id=peer(after(i)), device_id_type=MESH)
        return carry

    lax.fori_loop(1, chips, tell, 0)
    pl.semaphore_signal(barrier, inc=1, device_id=near, device_id_type=MESH)
    pl.semaphore_signal(barrier, inc=1, device_id=twin, device_id_type=MESH)

    own_rate, own_weight = rate_ref[...], weight_ref[...]
    own_bias = jnp.broadcast_to(bias_ref[...], (HALF, W))
    own_bias = jnp.concatenate([own_bias, pltpu.roll(own_bias, W // 2, 1)], axis=1)
    own_bias = [own_bias[:1], pltpu.roll(own_bias, W, 1)[:1]]
    lower = lambda z: z - z.astype(bf16).astype(f32)
    for half in range(2):
        rows = slice(quad * half, quad * half + quad)
        par[chip, half] = jnp.concatenate(
            [
                own_rate[rows],
                lower(own_rate)[rows],
                own_weight[rows],
                own_bias[half],
                lower(own_bias[half]),
                own_bias[1 - half],
                lower(own_bias[1 - half]),
            ],
            axis=0,
        ).astype(bf16)

    row_no = lax.broadcasted_iota(jnp.int32, (W, W), 0)
    lane_no = lax.broadcasted_iota(jnp.int32, (W, W), 1)
    fwd = tab_ref[...]
    flip = (row_no + lane_no == W - 1).astype(f32).astype(bf16)
    inv = (jnp.transpose(fwd) * (1.0 / W)).astype(bf16)
    fwd = fwd.astype(bf16)
    flip_ref[...] = flip
    fwd_ref[...] = fwd
    inv_ref[...] = inv
    fwdr_ref[...] = dot(flip, fwd).astype(bf16)
    invr_ref[...] = dot(inv, flip).astype(bf16)

    pieces = 4
    count = chips // pieces

    def products(order, dst, first):
        def step(i, carry):
            for v in [first + 4 * i + n for n in range(4)]:
                dst[0, v] = mul16(inp[order, 1, v], inp[order, 2, v]).reshape(W, W)
                dst[1, v] = mul16(inp[order, 3, v], inp[order, 0, v]).reshape(W, W)
            return carry

        lax.fori_loop(0, count // 4, step, 0)

    def send_par(i, carry):
        remote(
            par.at[chip], par.at[chip], par_sem.at[0], par_sem.at[1], peer(after(i))
        ).start()
        return carry

    wait_bytes(inp.at[0], load_sem.at[0])
    for n in range(pieces):
        products(0, away, n * count)
        if n == 0:
            pl.semaphore_wait(barrier, chips + 1)
            lax.fori_loop(1, chips, send_par, 0)
        block = pl.ds(n * count, count)
        remote(
            away.at[:, block], sig.at[core, :, block], pair_sem.at[pieces], pair_sem.at[n], near
        ).start()
    wait_bytes(inp.at[1], load_sem.at[1])
    for n in range(pieces):
        products(1, sig.at[core], n * count)

    eye = row_no == lane_no
    swapped_eye = lax.rem(row_no + W // 2, W) == lane_no
    lane = lax.broadcasted_iota(jnp.int32, (W, W), 1).astype(f32)
    mask = diag_mask()

    def local_lags(first, some):
        blocks = [first + n for n in range(some)]
        xs = [jnp.concatenate([sig[0, 0, v], sig[1, 0, v]], axis=0) for v in blocks]
        ms = [jnp.concatenate([sig[0, 1, v], sig[1, 1, v]], axis=0) for v in blocks]
        spec_x = [dot(x, fwd_ref[...]) for x in xs]
        spec_m = [dot(m, fwdr_ref[...]) for m in ms]
        turned = [dot(x, flip_ref[...]).astype(bf16) for x in xs]
        found = [dot(cmul(a, b), invr_ref[...]) for a, b in zip(spec_x, spec_m)]
        for n, v in enumerate(blocks):
            rev[0, v] = turned[n][:W]
            rev[1, v] = turned[n][W:]
            lag = found[n][:W] + found[n][W:]
            lags[0, v] = lag.astype(bf16)
            lags[1, v] = (lag * lane).astype(bf16)
            xm = xs[n].astype(f32) * ms[n].astype(f32)
            sums = jnp.sum(xm[:W] + xm[W:], axis=1, keepdims=True)
            for side, where in enumerate((eye, swapped_eye)):
                skip[v, HALF * side : HALF * side + HALF] = jnp.broadcast_to(
                    jnp.sum(jnp.where(where, sums, 0.0), axis=0, keepdims=True), (HALF, W)
                )

    def lags_of(half):
        for n in range(half * pieces // 2, (half + 1) * pieces // 2):
            block = pl.ds(n * count, count)
            wait_bytes(sig.at[core, :, block], pair_sem.at[n])
            local_lags(n * count, count)

    lags_of(0)
    lags_of(1)
    wait_bytes(par.at[pl.ds(0, chips - 1)], par_sem.at[1])

    def place(j, n):
        half = lax.div(j, steps)
        u = lax.rem(lax.div(chip, 2) + 2 * lax.rem(j, steps) + 1 + n, pairs)
        return half, u, half * pairs + u

    def halves(first, second, start):
        rows = slice(start, start + quad)
        return jnp.concatenate([first[rows], second[rows]], axis=0)

    def get_par(half, u):
        return par[2 * u, half].astype(f32), par[2 * u + 1, half].astype(f32)

    def get_rate(pair):
        return halves(*pair, 0) + halves(*pair, quad)

    def mode_sums(half, u, v):
        rate = get_rate(get_par(half, u))
        far = jnp.exp(-float(W) * rate)
        parts = [rev[0, v], rev[1, v], sig[0, 1, v], sig[1, 1, v], lags[0, v], lags[1, v]]
        for chunk in range(2):
            parts.append((parts[2 + chunk].astype(f32) * (lane + 1.0)).astype(bf16))
            parts.append((parts[chunk].astype(f32) * lane).astype(bf16))
        found = [[] for _ in parts]
        for g in range(HALF):
            e = powers(rate[g : g + 1])
            rows = slice(16 * g, 16 * g + 16)
            res = dot(jnp.concatenate([part[rows] for part in parts], axis=0), e)
            for n in range(len(parts)):
                found[n].append(diag_row(mask, res[16 * n : 16 * n + 16]))
        found = [jnp.concatenate(rows, axis=0) for rows in found]
        return found, found[0] * far + found[1], found[2] + far * found[3]

    def sum_step(j, carry):
        places = [place(j, n) for n in range(2)]
        results = [mode_sums(*where) for where in places]
        for (half, u, v), (found, ahead, back) in zip(places, results):
            for n, value in enumerate(found):
                keep[v, n] = value
            for n in range(2):
                rows = slice(quad * n, quad * n + quad)
                st_out[half, 2 * u + n] = jnp.concatenate([ahead[rows], back[rows]], axis=0)
        for half, u, v in places:
            for n in range(2):
                b = 2 * u + n

                @pl.when(b != chip)
                def _(b=b, half=half):
                    remote(
                        st_out.at[half, b], came.at[half, chip], st_sem.at[half, 0],
                        st_sem.at[half, 1], peer(b),
                    ).start()

        return carry

    def scan(half):
        came[half, chip] = st_out[half, chip]
        wait_bytes(came.at[half, pl.ds(0, chips - 1)], st_sem.at[half, 1])
        decay2 = jnp.exp(-2.0 * float(W) * own_rate[quad * half : quad * half + quad])

        def ahead(p, s):
            hold[p, 0:quad] = s
            return s * decay2 + came[half, p][:quad]

        lax.fori_loop(0, chips, ahead, jnp.zeros((quad, LANES), f32), unroll=8)

        def back(i, s):
            p = chips - 1 - i
            ready[half, p] = jnp.concatenate([hold[p, 0:quad], s], axis=0)
            return s * decay2 + came[half, p][quad:]

        lax.fori_loop(0, chips, back, jnp.zeros((quad, LANES), f32), unroll=8)

        def send_back(i, carry):
            b = after(i)
            remote(
                ready.at[half, b], got.at[half, chip], back_sem.at[half, 0], back_sem.at[half, 1],
                peer(b),
            ).start()
            return carry

        lax.fori_loop(1, chips, send_back, 0)
        got[half, chip] = ready[half, chip]

    def chunk_states(half, u, v, rate):
        pair = got[half, 2 * u], got[half, 2 * u + 1]
        far = jnp.exp(-float(W) * rate)
        s0, r1 = halves(*pair, 0), halves(*pair, quad)
        return s0, far * s0 + keep[v, 0], far * r1 + keep[v, 3], r1

    def send_grads(half):
        wait_bytes(got.at[half, pl.ds(0, chips - 1)], back_sem.at[half, 1])

        def made(u, v):
            rate = get_rate(get_par(half, u))
            near_decay = jnp.exp(-rate)
            s0, s1, r0, r1 = chunk_states(half, u, v, rate)
            grad_a = keep[v, 4] + near_decay * (keep[v, 2] * s0 + keep[v, 3] * s1)
            grad_d = keep[v, 5] + near_decay * (
                float(W) * jnp.exp(-float(W) * rate) * (s0 * r0 + s1 * r1)
                + s0 * keep[v, 6] + r0 * keep[v, 7] + s1 * keep[v, 8] + r1 * keep[v, 9]
            )
            messages = []
            for n in range(2):
                rows = slice(quad * n, quad * n + quad)
                first = 0 if n == half else HALF
                skip_part = jnp.concatenate(
                    [skip[v, first : first + HALF], jnp.zeros((HALF, W), f32)], axis=1
                )
                messages.append(
                    jnp.concatenate([grad_a[rows], grad_d[rows], skip_part], axis=0).astype(bf16)
                )
            return messages

        def step(i, carry):
            us = [lax.rem(lax.div(chip, 2) + 1 + 4 * i + n, pairs) for n in range(4)]
            results = [made(u, half * pairs + u) for u in us]
            for u, messages in zip(us, results):
                for n in range(2):
                    grad_out[half, 2 * u + n] = messages[n]
            for u in us:
                for n in range(2):
                    b = 2 * u + n

                    @pl.when(b != chip)
                    def _(b=b):
                        remote(
                            grad_out.at[half, b], grad_in.at[half, chip], grad_sem.at[half, 0],
                            grad_sem.at[half, 1], peer(b),
                        ).start()

            return carry

        lax.fori_loop(0, pairs // 4, step, 0)
        grad_in[half, chip] = grad_out[half, chip]

    def expand(half, u, v):
        pair = get_par(half, u)
        rate, weight = get_rate(pair), halves(*pair, 2 * quad)
        s0, s1, r0, r1 = chunk_states(half, u, v, rate)
        wa = weight * jnp.exp(-rate)
        terms = [weight, wa * s0, wa * s1, wa * r0, wa * r1]
        made = []
        for g in range(HALF):
            e = powers(rate[g : g + 1])
            lhs = jnp.concatenate(
                [jnp.where(mask, term[g : g + 1], 0.0) for term in terms], axis=0
            ).astype(bf16)
            made.append(dot_nt(lhs, e))
        return [jnp.concatenate([z[16 * n : 16 * n + 16] for z in made], axis=0) for n in range(5)]

    def convolve(half, u, v, taps, y0, y1, p0, p1):
        pair = get_par(half, u)
        even, odd = pair[0][12:13, :W] + pair[0][13:14, :W], pair[1][14:15, :W] + pair[1][15:, :W]
        bias_row = jnp.where(lane[:1] < W // 2, even, odd)
        x = jnp.concatenate([sig[0, 0, v], sig[1, 0, v]], axis=0)
        m = jnp.concatenate([sig[0, 1, v], sig[1, 1, v]], axis=0)
        spec_x, spec_m = dot(x, fwd_ref[...]), dot(m, fwdr_ref[...])
        spec_h = dot(taps.astype(bf16), fwd_ref[...])
        spec_h = jnp.concatenate([spec_h, spec_h], axis=0)
        gain = jnp.sum(jnp.where(eye, bias_row, 0.0), axis=1, keepdims=True)
        gain = jnp.concatenate([gain, gain], axis=0)
        y = dot(cmul(spec_x, spec_h), inv_ref[...])
        y += jnp.concatenate([y0, y1], axis=0) + gain * x.astype(f32)
        p = dot(cmul(spec_m, spec_h), invr_ref[...])
        p += dot(jnp.concatenate([p0, p1], axis=0).astype(bf16), flip_ref[...])
        p += gain * m.astype(f32)
        return y.astype(bf16), p.astype(bf16)

    def finish(j, carry):
        places = [place(j, n) for n in range(2)]
        grown = [expand(*where) for where in places]
        results = [convolve(*where, *terms) for where, terms in zip(places, grown)]
        for (half, u, v), result in zip(places, results):
            for n, out in enumerate((mixed_ref, pgrad_ref)):
                both = [
                    result[n][W * chunk : W * chunk + W].reshape(2, W // 2, W) for chunk in range(2)
                ]
                mine_first = core == 0
                kept = jnp.where(mine_first, both[0], both[1])
                stage[n, v] = jnp.where(mine_first, both[1], both[0])
                for side in range(2):
                    out[u, side, core, half] = kept[side]
        for half, u, v in places:
            for n, out in enumerate((mixed_ref, pgrad_ref)):
                remote(
                    stage.at[n, v], out.at[u, :, core, half], out_sem.at[0], out_sem.at[1], near
                ).start()
        return carry

    middle = steps + 5 * steps // 8
    lax.fori_loop(0, steps, sum_step, 0)
    lax.fori_loop(steps, middle, sum_step, 0)
    scan(0)
    lax.fori_loop(middle, 2 * steps, sum_step, 0)
    send_grads(0)
    lax.fori_loop(0, steps // 4, finish, 0)
    scan(1)
    lax.fori_loop(steps // 4, steps, finish, 0)
    send_grads(1)
    early = steps + 3 * steps // 4
    lax.fori_loop(steps, early, finish, 0)
    for half in range(2):
        wait_bytes(grad_in.at[half, pl.ds(0, chips - 1)], grad_sem.at[half, 1])
        mine[half] = lax.fori_loop(
            0, chips, lambda p, t: t + grad_in[half, p].astype(f32), jnp.zeros((16, LANES), f32),
            unroll=8,
        )
    swap = remote(mine, theirs, twin_sem.at[0], twin_sem.at[1], twin)
    swap.start()
    lax.fori_loop(early, 2 * steps, finish, 0)
    wait_bytes(away, pair_sem.at[pieces])
    wait_bytes(par.at[pl.ds(0, chips - 1)], par_sem.at[0])
    for half in range(2):
        wait_bytes(st_out.at[half, pl.ds(0, chips - 1)], st_sem.at[half, 0])
        wait_bytes(ready.at[half, pl.ds(0, chips - 1)], back_sem.at[half, 0])
        wait_bytes(grad_out.at[half, pl.ds(0, chips - 1)], grad_sem.at[half, 0])
    for n in range(2):
        wait_bytes(stage, out_sem.at[n])
    swap.wait()
    total_ref[...] = mine[...] + theirs[...]


def body(query, key_in, value_in, cotangent, residue, log_rate, bias):
    shards = lax.axis_size("ctx")
    channels, width = query.shape
    rate = jnp.exp(log_rate)
    root = jnp.sqrt(-jnp.expm1(-2.0 * rate))
    rate_rows = rate.reshape(HALF, LANES)
    weight_rows = (residue * root).reshape(HALF, LANES)
    vmem = pl.BlockSpec(memory_space=pltpu.VMEM)
    dma = pltpu.SemaphoreType.DMA

    def remote(number):
        return pltpu.CompilerParams(
            collective_id=number, has_side_effects=True, vmem_limit_bytes=49 * 1024 * 1024
        )

    chips = shards // 2
    split = lambda z: z.reshape(chips // 2, 2, 2, 2, W // 2, width)
    anywhere = pl.BlockSpec(memory_space=pl.ANY)
    part = jax.ShapeDtypeStruct((chips // 2, 2, 2, 2, W // 2, width), bf16)
    mixed, pgrad, total = pl.pallas_call(
        mixer_kernel,
        in_specs=[anywhere] * 4 + [vmem] * 4,
        out_specs=[vmem] * 3,
        out_shape=[part, part, jax.ShapeDtypeStruct((2, 16, LANES), f32)],
        scratch_shapes=[
            pltpu.VMEM((W, 2 * W), bf16),
            pltpu.VMEM((W, 2 * W), bf16),
            pltpu.VMEM((2 * W, W), bf16),
            pltpu.VMEM((2 * W, W), bf16),
            pltpu.VMEM((W, W), bf16),
            pltpu.VMEM((2, 4, chips, 2, W // 2, W), bf16),
            pltpu.VMEM((2, chips, W, W), bf16),
            pltpu.VMEM((2, 2, chips, W, W), bf16),
            pltpu.VMEM((2, chips, W, W), bf16),
            pltpu.VMEM((2, chips, W, W), bf16),
            pltpu.VMEM((chips, 2 * HALF, W), f32),
            pltpu.VMEM((chips, 2, 16, LANES), bf16),
            pltpu.VMEM((chips, 10, HALF, LANES), f32),
            pltpu.VMEM((2, chips, HALF, LANES), f32),
            pltpu.VMEM((2, chips, HALF, LANES), f32),
            pltpu.VMEM((chips, HALF, LANES), f32),
            pltpu.VMEM((2, chips, HALF, LANES), f32),
            pltpu.VMEM((2, chips, HALF, LANES), f32),
            pltpu.VMEM((2, chips, 16, LANES), bf16),
            pltpu.VMEM((2, chips, 16, LANES), bf16),
            pltpu.VMEM((2, 16, LANES), f32),
            pltpu.VMEM((2, 16, LANES), f32),
            pltpu.VMEM((2, chips, 2, W // 2, W), bf16),
            dma((2,)),
            dma((2,)),
            dma((5,)),
            dma((2, 2)),
            dma((2, 2)),
            dma((2, 2)),
            dma((2,)),
            dma((2,)),
        ],
        compiler_params=remote(1),
        name="mixer",
    )(split(query), split(key_in), split(value_in), split(cotangent), table(), rate_rows,
      weight_rows, bias.reshape(1, W))
    mixed = mixed.reshape(channels, width)
    pgrad = pgrad.reshape(channels, width)
    gated, gq = mul16(query, mixed), mul16(cotangent, mixed)
    gk, gv = mul16(pgrad, value_in), mul16(pgrad, key_in)

    modes = residue.shape[1]
    quad = HALF // 2
    grad_a = total[:, :quad].reshape(-1, modes)
    grad_d = total[:, quad : 2 * quad].reshape(-1, modes)
    skip = jnp.concatenate([total[0, HALF, : W // 2], total[1, HALF, W // 2 : W]])
    scale = 1.0 / math.sqrt(float(shards * width * lax.axis_size("dp")))
    grad_residue = root * grad_a * scale
    grad_rate = rate * residue * (jnp.exp(-2.0 * rate) / root * grad_a - root * grad_d) * scale
    grad_bias = skip * scale
    return gated, gq, gk, gv, grad_residue, grad_rate, grad_bias


def solution(mesh):
    tok = P(None, ("dp", "ctx"))
    chan = P("ctx", None)
    return jax.shard_map(
        body,
        mesh=mesh,
        in_specs=(tok, tok, tok, tok, chan, chan, P("ctx")),
        out_specs=(tok, tok, tok, tok, chan, chan, P("ctx")),
        check_vma=False,
    )
```
